128 devices in a mesh: eblock: 16 (over z, y), dom: 8 (over x, core).
Axes of the slice: x: 4, y: 4, z: 4, core: 2. Of those that a mesh axis runs over, the one named last changes fastest.
Arguments:
- table: bfloat16 [131072, 512], P(('eblock', 'dom')), may hold values from -1.25 to 1.25
- requests: int32 [16, 8, 8, 128], P('eblock', 'dom'), may hold values from -1 to 1023, as said below
- edge_src: int32 [16, 8, 2048], P('eblock', 'dom'), may hold values from 0 to 1023, as said below
- edge_dst: int32 [16, 8, 2048], P('eblock', 'dom'), may hold values from 0 to 1023, as said below
- labels: int32 [16, 8, 2048], P('eblock', 'dom'), may hold values 0 or 1
- neg_ids: int32 [16, 8, 128], P('eblock', 'dom'), may hold values from 0 to 1023
Outputs:
- table_grad: float32 [131072, 512], P(('eblock', 'dom'))
The draws below stay inside these ranges and needn't reach their ends.
Inputs may be any that keep to these rules, and one draw needn't show every extreme that they name: `requests`: in each block of 128 the live entries come first and are distinct; each device has full blocks, one of them to master 8 - 1. `edge_src`: every slot names a live entry of the device's requests. `edge_dst`: every slot names a live entry of the device's requests.
All inputs are finite; a program needn't handle non-finite values. No bound on the sum of `labels` on one device may be relied on, other than what follows from the above.
Results may differ from the reference program's by a relative error of at most 0.0017.
Values may be sent and summed in bfloat16 or wider, within the bound.
A program may use at most 128 MiB of HBM per device.

```python
import jax
import jax.numpy as jnp
from jax import lax

D = 512
R = 128
EDEV = 2048
NEG = 128
VDEV = 1024
VERTS = 131072
N_EBLOCK = 16
N_DOM = 8


def request_counts(key):
    filled = jax.random.randint(key, (N_EBLOCK, N_DOM, N_DOM), R // 4, R + 1)
    e_index = jnp.arange(N_EBLOCK)[:, None, None]
    d_index = jnp.arange(N_DOM)[None, :, None]
    p_index = jnp.arange(N_DOM)[None, None, :]
    full = (p_index == (d_index + e_index) % N_DOM) | (p_index == N_DOM - 1)
    return jnp.where(full, R, filled).astype(jnp.int32)


def edge_slots(key, counts):
    first, second = jax.random.split(key)
    peer = jax.random.randint(first, (N_EBLOCK, N_DOM, EDEV), 0, N_DOM)
    bound = jnp.take_along_axis(counts, peer, axis=2)
    place = jax.random.randint(second, (N_EBLOCK, N_DOM, EDEV), 0, bound)
    slots = peer * R + place
    return slots.at[:, :, 0].set((N_DOM - 1) * R + R - 1).astype(jnp.int32)


def draw_requests(key, part):
    counts = request_counts(key)
    key = jax.random.fold_in(key, 11)
    keys = jax.random.split(key, N_EBLOCK * N_DOM * N_DOM)
    chosen = jax.vmap(lambda k: jax.random.permutation(k, VDEV)[:R])(keys)
    chosen = chosen.reshape(N_EBLOCK, N_DOM, N_DOM, R)
    places = jnp.arange(R)[None, None, None, :]
    return jnp.where(places < counts[..., None], chosen, -1).astype(jnp.int32)


def draw_edge_src(key, part):
    counts = request_counts(key)
    key = jax.random.fold_in(key, 12)
    return edge_slots(key, counts)


def draw_edge_dst(key, part):
    counts = request_counts(key)
    key = jax.random.fold_in(key, 13)
    return edge_slots(key, counts)


def place_ends(drawn, stream_key, smallest, largest):
    longest = drawn.shape.index(max(drawn.shape))
    spots = []
    for shift in (0, 1):
        where = [jax.random.randint(jax.random.fold_in(stream_key, axis), (), 0, length) for axis, length in enumerate(drawn.shape)]
        where[longest] = (where[longest] + shift) % drawn.shape[longest]
        spots.append(tuple(where))
    return drawn.at[spots[0]].set(smallest).at[spots[1]].set(largest)


def block_levels(own_key, shape, cuts, low, largest):
    loudness = 1.0
    for position, blocks in cuts:
        heights = jax.random.uniform(jax.random.fold_in(jax.random.fold_in(own_key, 6), position), (blocks,), jnp.float32, low / len(cuts), largest / len(cuts))
        loudness = loudness * jnp.repeat(jnp.exp(heights), shape[position] // blocks).reshape((-1,) + (1,) * (len(shape) - 1 - position))
    return loudness


def bell_draw(key, shape, scale, most, pieces=(), kind=jnp.bfloat16):
    array = jax.random.normal(key, shape, jnp.float32) * scale
    if len(pieces) > 0:
        array = block_levels(key, shape, pieces, -0.22, 0.18) * array
    return jnp.clip(array, min=-most, max=most).astype(kind)


def setup_inputs(seed: int = 0) -> dict:
    key_of = jax.random.split(jax.random.key(seed), 7)
    table = bell_draw(key_of[0], (VERTS, D), 0.21, 1.25, ((0, 128),))
    requests = draw_requests(jax.random.fold_in(key_of[6], 71), 0)
    edge_src = draw_edge_src(jax.random.fold_in(key_of[6], 71), 0)
    edge_dst = draw_edge_dst(jax.random.fold_in(key_of[6], 71), 0)
    labels = place_ends((jax.random.randint(key_of[4], (N_EBLOCK, N_DOM, EDEV), 0, 2) < 1).astype(jnp.int32), jax.random.fold_in(key_of[4], 1), 0, 1)
    neg_ids = place_ends(jax.random.randint(key_of[5], (N_EBLOCK, N_DOM, NEG), 0, VDEV), jax.random.fold_in(key_of[5], 1), 0, VDEV - 1).astype(jnp.int32)
    return {"table": table, "requests": requests, "edge_src": edge_src, "edge_dst": edge_dst, "labels": labels, "neg_ids": neg_ids}


def reference(table, requests, edge_src, edge_dst, labels, neg_ids):
    shards = table.reshape(N_EBLOCK, N_DOM, VDEV, D)
    live = requests >= 0
    safe = jnp.maximum(requests, 0)
    e_index = jnp.arange(N_EBLOCK)[:, None, None, None]
    p_index = jnp.arange(N_DOM)[None, None, :, None]
    rows = shards[e_index, p_index, safe]
    rows = jnp.where(live[..., None], rows, jnp.zeros((), jnp.bfloat16))
    neg_rows = shards[jnp.arange(N_EBLOCK)[:, None, None], jnp.arange(N_DOM)[None, :, None], neg_ids]
    weight = 1.0 / N_EBLOCK
    targets = jnp.where(live, jnp.arange(N_DOM)[None, None, :, None] * VDEV + safe, N_DOM * VDEV)

    def one_device(carry, which):
        grads, negative_grads = carry
        e_pos = which // N_DOM
        d_pos = which % N_DOM
        slots = rows[e_pos, d_pos].reshape(N_DOM * R, D)
        src_ids = edge_src[e_pos, d_pos]
        dst_ids = edge_dst[e_pos, d_pos]
        source = slots[src_ids]
        target = slots[dst_ids]
        cand = lax.dynamic_index_in_dim(neg_rows, d_pos, 1, keepdims=False).reshape(N_EBLOCK * NEG, D)
        pos = jnp.sum(source.astype(jnp.float32) * target.astype(jnp.float32), axis=1)
        dpos = jax.nn.sigmoid(pos) - labels[e_pos, d_pos].astype(jnp.float32)
        scores = jnp.dot(source, cand.T, preferred_element_type=jnp.float32)
        dneg = (weight * jax.nn.sigmoid(scores)).astype(jnp.bfloat16)
        gsrc = jnp.dot(dneg, cand, preferred_element_type=jnp.float32) + dpos[:, None] * target.astype(jnp.float32)
        gdst = dpos[:, None] * source.astype(jnp.float32)
        slot_grad = jax.ops.segment_sum(gsrc, src_ids, N_DOM * R) + jax.ops.segment_sum(gdst, dst_ids, N_DOM * R)
        gcand = jnp.dot(dneg.T, source, preferred_element_type=jnp.float32).reshape(N_EBLOCK, NEG, D)
        added = jax.ops.segment_sum(slot_grad, targets[e_pos, d_pos].reshape(-1), N_DOM * VDEV + 1)[:-1]
        grads = grads.at[e_pos].add(added.reshape(N_DOM, VDEV, D))
        negative_grads = negative_grads.at[:, d_pos].add(gcand)
        return (grads, negative_grads), None

    start = (jnp.zeros((N_EBLOCK, N_DOM, VDEV, D), jnp.float32), jnp.zeros((N_EBLOCK, N_DOM, NEG, D), jnp.float32))
    (grads, negative_grads), _ = lax.scan(one_device, start, jnp.arange(N_EBLOCK * N_DOM).astype(jnp.int32))
    extra = jax.vmap(jax.vmap(lambda g, i: jax.ops.segment_sum(g, i, VDEV)))(negative_grads, neg_ids)
    return (grads + extra).reshape(VERTS, D)
```

```python
import jax
import jax.numpy as jnp
from jax import lax
from jax.experimental import pallas as pl
from jax.experimental.pallas import tpu as pltpu
from jax.sharding import PartitionSpec as P

MESH = pl.DeviceIdType.MESH
BF = jnp.bfloat16
F32 = jnp.float32
D = 512
R = 128
S = 1024
E = 2048
C = 2048
V = 1024
H = 64
LABEL = 4096.0

DOM = ((2, 0), (2, 1), (1, 0), (1, 1), (3, 0), (3, 1), (0, 1))
RING = (2, 1, 3)


def nt(a, b):
    return lax.dot_general(a, b, (((1,), (1,)), ((), ())), preferred_element_type=F32)


def nn(a, b):
    return jnp.dot(a, b, preferred_element_type=F32)


def onehot_rows(ids, count):
    column = jnp.transpose(ids)[:, :1]
    return jnp.where(lax.broadcasted_iota(jnp.int32, (R, count), 1) == column, 1.0, 0.0).astype(BF)


def onehot_columns(ids, count, base=0):
    place = lax.broadcasted_iota(jnp.int32, (count, ids.shape[1]), 0) + base
    return jnp.where(place == ids, 1.0, 0.0).astype(BF)


def rows(i, n):
    return pl.ds(pl.multiple_of(i * n, n), n)


def kernel(
    table_hbm, req_ref, src_ref, dst_ref, lab_ref, neg_ref, out_ref,
    table, reqst, asked, picked, slots, cslots, cand, dnt, st, wt, cnt, lbl, cdeg, gneg, gst, ret, xt,
    gca, gcown, rs1, part, rs2,
    tab_sem, s_req, r_req, s_slot, r_slot, s_ag1, r_ag1, s_ag2, r_ag2, s_ret, r_ret, s_rs1, r_rs1, s_rs2, r_rs2,
):
    e = lax.axis_index("eblock")
    d = lax.axis_index("dom")
    z, y = lax.div(e, 4), lax.rem(e, 4)
    x, c = lax.div(d, 2), lax.rem(d, 2)

    def plus(a, by, n=4):
        return lax.rem(a + by, n)

    def dom_peer(dx, dc):
        return plus(x, dx) * 2 + plus(c, dc, 2)

    def along(half, by):
        if half == 0:
            return (z * 4 + plus(y, by), d)
        return (plus(z, by) * 4 + y, d)

    def across(half, by):
        return along(1 - half, by)

    outer = (z, y)
    inner = (y, z)

    def remote(src, dst, ssem, rsem, to):
        return pltpu.make_async_remote_copy(
            src_ref=src, dst_ref=dst, send_sem=ssem, recv_sem=rsem, device_id=to, device_id_type=MESH
        )

    barrier = pltpu.get_barrier_semaphore()
    for dx, dc in DOM:
        pl.semaphore_signal(barrier, inc=1, device_id=(e, dom_peer(dx, dc)), device_id_type=MESH)
    for half in range(2):
        for by in RING:
            pl.semaphore_signal(barrier, inc=1, device_id=along(half, by), device_id_type=MESH)

    load = pltpu.make_async_copy(table_hbm, table, tab_sem)
    load.start()
    for p in range(8):
        reqst[p] = jnp.broadcast_to(req_ref[p : p + 1, :], (8, R))
    neg = jnp.broadcast_to(neg_ref[...], (8, R))
    neg_hot = onehot_rows(neg, V)
    pl.semaphore_wait(barrier, 13)

    req_cp = []
    for i, (dx, dc) in enumerate(DOM):
        peer = dom_peer(dx, dc)
        cp = remote(reqst.at[peer], asked.at[d], s_req.at[i], r_req.at[i], (e, peer))
        cp.start()
        req_cp.append(cp)
    asked[d] = reqst[d]

    load.wait()
    own = nn(neg_hot, table[...]).astype(BF)
    ag1 = []
    for half in range(2):
        at = rows(half * 16 + outer[half] * 4 + inner[half], H)
        cand[at, :] = own[half * H : (half + 1) * H, :]
        for i, by in enumerate(RING):
            cp = remote(cand.at[at], cand.at[at], s_ag1.at[half * 3 + i], r_ag1.at[half * 3 + i], along(half, by))
            cp.start()
            ag1.append(cp)

    for cp in req_cp:
        cp.wait_recv()
    slot_cp = []
    for dx in (2, 1, 3, 0):
        base = plus(x, dx) * 2
        hot = jnp.concatenate([onehot_rows(asked[base], V), onehot_rows(asked[base + 1], V)], axis=0)
        picked[rows(plus(x, dx), 2 * R), :] = nn(hot, table[...]).astype(BF)
        for dc in range(2):
            if (dx, dc) == (0, 0):
                continue
            i = DOM.index((dx, dc))
            peer = dom_peer(dx, dc)
            cp = remote(picked.at[rows(peer, R)], slots.at[rows(d, R)], s_slot.at[i], r_slot.at[i], (e, peer))
            cp.start()
            slot_cp.append(cp)
    slots[rows(d, R), :] = picked[rows(d, R), :]

    for cp in ag1:
        cp.wait_recv()
    ag2 = []
    for half in range(2):
        at = rows(half * 4 + outer[half], 4 * H)
        for i, by in enumerate(RING):
            cp = remote(cand.at[at], cand.at[at], s_ag2.at[half * 3 + i], r_ag2.at[half * 3 + i], across(half, by))
            cp.start()
            ag2.append(cp)

    weight = jnp.where(lab_ref[...] == 1, LABEL, 1.0)

    @pl.loop(0, 8)
    def _(t):
        at = rows(t, R)
        place = lax.broadcasted_iota(jnp.int32, (R, E), 0) + t * R
        hot = jnp.where(place == src_ref[...], 1.0, 0.0)
        st[at, :] = hot.astype(BF)
        cdeg[at, :] = jnp.broadcast_to(jnp.sum(hot, axis=1, keepdims=True), (R, R))
        wt[at, :] = jnp.where(place == dst_ref[...], weight, 0.0).astype(BF)
        xt[:, at] = onehot_columns(asked[t][:1, :], V)

    neg_cols = onehot_columns(neg_ref[...], V)
    xt[:, S : S + R] = neg_cols
    xt[:, S + R : S + 2 * R] = neg_cols

    @pl.loop(0, 16)
    def _(t):
        a = rows(lax.div(t, 4), 256)
        b = rows(lax.rem(t, 4), 256)
        one = nt(st[a, :], wt[b, :])
        two = nt(wt[a, :], st[b, :])
        ones = jnp.floor(one * (1.0 / LABEL)) + jnp.floor(two * (1.0 / LABEL))
        lbl[a, b] = ones
        cnt[a, b] = one + two - (LABEL - 1.0) * ones

    for cp in ag2:
        cp.wait_recv()
    for dx in (0, 1, 3, 2):
        for dc in range(2):
            if (dx, dc) != (0, 0):
                slot_cp[DOM.index((dx, dc))].wait_recv()
        q = plus(x, 4 - dx)
        at = rows(q, 256)
        cslots[at, :] = (slots[at, :].astype(F32) * cdeg[at, :1]).astype(BF)

        @pl.loop(0, 4)
        def _(t):
            block = rows(t, 512)
            there = nt(slots[at, :], cand[block, :])
            dneg = (jnp.tanh(there * 0.5) * (1.0 / 32) + (1.0 / 32)).astype(BF)
            more = nn(dneg, cand[block, :])

            @pl.when(t == 0)
            def _():
                gneg[at, :] = more

            @pl.when(t > 0)
            def _():
                gneg[at, :] += more

            turned = nt(cand[block, :], slots[at, :])
            dnt[block, at] = (jnp.tanh(turned * 0.5) * (1.0 / 32) + (1.0 / 32)).astype(BF)

    ret_cp = []
    rs_cp = []

    def slot_grads(dx):
        q = plus(x, dx)
        at = rows(q, 256)
        gneg[at, :] = gneg[at, :] * cdeg[at, :1]

        @pl.loop(0, 4)
        def _(t):
            block = rows(t, 256)
            pos = nt(slots[at, :], slots[block, :])
            w = cnt[at, block] * (jnp.tanh(pos * 0.5) * 0.5 + 0.5) - lbl[at, block]
            gneg[at, :] += nn(w.astype(BF), slots[block, :])

        gst[at, :] = gneg[at, :].astype(BF)
        for dc in range(2):
            if (dx, dc) == (0, 0):
                ret[rows(d, R), :] = gst[rows(d, R), :]
                continue
            i = DOM.index((dx, dc))
            peer = dom_peer(dx, dc)
            cp = remote(gst.at[rows(peer, R)], ret.at[rows(d, R)], s_ret.at[i], r_ret.at[i], (e, peer))
            cp.start()
            ret_cp.append(cp)

    def cand_grads(by):
        for half in range(2):
            at = rows(half * 4 + plus(outer[half], by), 4 * H)
            total = nn(dnt[at, :], cslots[...])
            if by == 0:
                gcown[half] = total
            else:
                i = half * 3 + RING.index(by)
                gca[i] = total.astype(BF)
                cp = remote(gca.at[i], rs1.at[i], s_rs1.at[i], r_rs1.at[i], across(half, by))
                cp.start()
                rs_cp.append(cp)

    for by in (2, 1, 3, 0):
        slot_grads(by)
        cand_grads(by)

    for cp in rs_cp:
        cp.wait_recv()
    rs2_cp = []
    for half in range(2):
        total = gcown[half]
        for i in range(3):
            total = total + rs1[half * 3 + i].astype(F32)
        part[half] = total
        for i, by in enumerate(RING):
            k = half * 3 + i
            cp = remote(
                part.at[half, rows(plus(inner[half], by), H)], rs2.at[k], s_rs2.at[k], r_rs2.at[k], along(half, by)
            )
            cp.start()
            rs2_cp.append(cp)
    for cp in ret_cp:
        cp.wait_recv()
    for cp in rs2_cp:
        cp.wait_recv()
    for half in range(2):
        total = part[half, rows(inner[half], H), :]
        for i in range(3):
            total = total + rs2[half * 3 + i]
        high = total.astype(BF)
        ret[S + half * H : S + (half + 1) * H, :] = high
        ret[S + R + half * H : S + R + (half + 1) * H, :] = (total - high.astype(F32)).astype(BF)

    @pl.loop(0, 4)
    def _(t):
        at = rows(t, 256)
        out_ref[at, :] = nn(xt[at, :], ret[...])

    for cp in req_cp + ag1 + ag2 + slot_cp + ret_cp + rs_cp + rs2_cp:
        cp.wait_send()


def local(table, requests, edge_src, edge_dst, labels, neg_ids):
    vmem = pl.BlockSpec(memory_space=pltpu.VMEM)
    dma = pltpu.SemaphoreType.DMA
    return pl.pallas_call(
        kernel,
        out_shape=jax.ShapeDtypeStruct((V, D), F32),
        in_specs=[pl.BlockSpec(memory_space=pl.ANY)] + [vmem] * 5,
        out_specs=vmem,
        scratch_shapes=[
            pltpu.VMEM((V, D), BF),
            pltpu.VMEM((8, 8, R), jnp.int32),
            pltpu.VMEM((8, 8, R), jnp.int32),
            pltpu.VMEM((S, D), BF),
            pltpu.VMEM((S, D), BF),
            pltpu.VMEM((S, D), BF),
            pltpu.VMEM((C, D), BF),
            pltpu.VMEM((C, S), BF),
            pltpu.VMEM((S, E), BF),
            pltpu.VMEM((S, E), BF),
            pltpu.VMEM((S, S), F32),
            pltpu.VMEM((S, S), F32),
            pltpu.VMEM((S, R), F32),
            pltpu.VMEM((S, D), F32),
            pltpu.VMEM((S, D), BF),
            pltpu.VMEM((S + 2 * R, D), BF),
            pltpu.VMEM((V, S + 2 * R), BF),
            pltpu.VMEM((6, 4 * H, D), BF),
            pltpu.VMEM((2, 4 * H, D), F32),
            pltpu.VMEM((6, 4 * H, D), BF),
            pltpu.VMEM((2, 4 * H, D), F32),
            pltpu.VMEM((6, H, D), F32),
            dma,
            dma((7,)), dma((7,)),
            dma((7,)), dma((7,)),
            dma((6,)), dma((6,)),
            dma((6,)), dma((6,)),
            dma((7,)), dma((7,)),
            dma((6,)), dma((6,)),
            dma((6,)), dma((6,)),
        ],
        compiler_params=pltpu.CompilerParams(
            collective_id=0, has_side_effects=True, vmem_limit_bytes=56 * 1024 * 1024
        ),
        name="link_step",
    )(
        table,
        requests.reshape(8, R),
        edge_src.reshape(1, E),
        edge_dst.reshape(1, E),
        labels.reshape(1, E),
        neg_ids.reshape(1, R),
    )


def solution(mesh):
    return jax.shard_map(
        local,
        mesh=mesh,
        in_specs=(
            P(("eblock", "dom"), None),
            P("eblock", "dom", None, None),
            P("eblock", "dom", None),
            P("eblock", "dom", None),
            P("eblock", "dom", None),
            P("eblock", "dom", None),
        ),
        out_specs=P(("eblock", "dom"), None),
        check_vma=False,
    )
```

```python
import jax
import jax.numpy as jnp
from jax import lax
from jax.experimental import pallas as pl
from jax.experimental.pallas import tpu as pltpu
from jax.sharding import PartitionSpec as P

MESH = pl.DeviceIdType.MESH
BF = jnp.bfloat16
F32 = jnp.float32
D = 512
R = 128
S = 1024
E = 2048
C = 2048
V = 1024
H = 64
LABEL = 4096.0

DOM = ((2, 0), (2, 1), (1, 0), (1, 1), (3, 0), (3, 1), (0, 1))
RING = (2, 1, 3)


def nt(a, b):
    return lax.dot_general(a, b, (((1,), (1,)), ((), ())), preferred_element_type=F32)


def nn(a, b):
    return jnp.dot(a, b, preferred_element_type=F32)


def onehot_rows(ids, count):
    column = jnp.transpose(ids)[:, :1]
    return jnp.where(lax.broadcasted_iota(jnp.int32, (R, count), 1) == column, 1.0, 0.0).astype(BF)


def onehot_columns(ids, count, base=0):
    place = lax.broadcasted_iota(jnp.int32, (count, ids.shape[1]), 0) + base
    return jnp.where(place == ids, 1.0, 0.0).astype(BF)


def rows(i, n):
    return pl.ds(pl.multiple_of(i * n, n), n)


def step_kernel(
    table_hbm, req_ref, src_ref, dst_ref, lab_ref, neg_ref, ret, asked_out, neg_out,
    table, reqst, asked, picked, slots, cslots, cand, dnt, st, wt, cnt, off, cdeg, selfw, gneg, gst,
    opp, side, kept, gcown, rly, rs1, part, rs2,
    tab_sem, own_sem, s_req, r_req, s_slot, r_slot, s_ag1, r_ag1, s_ag2, r_ag2, s_ret, r_ret, s_rs1, r_rs1, s_rs2, r_rs2,
):
    e = lax.axis_index("eblock")
    d = lax.axis_index("dom")
    z, y = lax.div(e, 4), lax.rem(e, 4)
    x, c = lax.div(d, 2), lax.rem(d, 2)

    def plus(a, by, n=4):
        return lax.rem(a + by, n)

    def dom_peer(dx, dc):
        return plus(x, dx) * 2 + plus(c, dc, 2)

    def along(half, by):
        if half == 0:
            return (z * 4 + plus(y, by), d)
        return (plus(z, by) * 4 + y, d)

    def across(half, by):
        return along(1 - half, by)

    outer = (z, y)
    inner = (y, z)

    def group(half, by, first=0, count=4 * H):
        start = (half * 4 + plus(outer[half], by)) * (4 * H) + first
        return pl.ds(pl.multiple_of(start, count), count)

    def remote(src, dst, ssem, rsem, to):
        return pltpu.make_async_remote_copy(
            src_ref=src, dst_ref=dst, send_sem=ssem, recv_sem=rsem, device_id=to, device_id_type=MESH
        )

    barrier = pltpu.get_barrier_semaphore()
    for dx, dc in DOM:
        pl.semaphore_signal(barrier, inc=1, device_id=(e, dom_peer(dx, dc)), device_id_type=MESH)
    for half in range(2):
        for by in RING:
            pl.semaphore_signal(barrier, inc=1, device_id=along(half, by), device_id_type=MESH)

    load = pltpu.make_async_copy(table_hbm, table, tab_sem)
    load.start()
    for p in range(8):
        reqst[p] = jnp.broadcast_to(req_ref[p : p + 1, :], (8, R))
    neg_hot = onehot_rows(jnp.broadcast_to(neg_ref[...], (8, R)), V)
    pl.semaphore_wait(barrier, 13)

    req_cp = []
    for i, (dx, dc) in enumerate(DOM):
        peer = dom_peer(dx, dc)
        cp = remote(reqst.at[peer], asked.at[d], s_req.at[i], r_req.at[i], (e, peer))
        cp.start()
        req_cp.append(cp)
    asked[d] = reqst[d]

    load.wait()
    own = (nn(neg_hot, table[...]) * 0.5).astype(BF)
    ag1 = []
    for half in range(2):
        at = rows(half * 16 + outer[half] * 4 + inner[half], H)
        cand[at, :] = own[half * H : (half + 1) * H, :]
        for i, by in enumerate(RING):
            cp = remote(cand.at[at], cand.at[at], s_ag1.at[half * 3 + i], r_ag1.at[half * 3 + i], along(half, by))
            cp.start()
            ag1.append(cp)

    slot_cp = [None] * 7
    for dx in (2, 1, 3, 0):
        for dc in range(2):
            if (dx, dc) != (0, 0):
                req_cp[DOM.index((dx, dc))].wait_recv()
    for dx in (2, 1, 3, 0):
        base = plus(x, dx) * 2
        hot = jnp.concatenate([onehot_rows(asked[base], V), onehot_rows(asked[base + 1], V)], axis=0)
        picked[rows(plus(x, dx), 2 * R), :] = nn(hot, table[...]).astype(BF)
        for dc in range(2):
            if (dx, dc) == (0, 0):
                continue
            i = DOM.index((dx, dc))
            peer = dom_peer(dx, dc)
            cp = remote(picked.at[rows(peer, R)], slots.at[rows(d, R)], s_slot.at[i], r_slot.at[i], (e, peer))
            cp.start()
            slot_cp[i] = cp
    slots[rows(d, R), :] = picked[rows(d, R), :]

    for cp in ag1:
        cp.wait_recv()
    ag2 = {}

    def gather_step(half, k, to, by, first):
        at = group(half, by, first, 2 * H)
        cp = remote(cand.at[at], cand.at[at], s_ag2.at[half * 6 + k], r_ag2.at[half * 6 + k], across(half, to))
        cp.start()
        ag2[half, k] = cp

    for half in range(2):
        gather_step(half, 0, 1, 0, 0)
        gather_step(half, 1, 3, 0, 2 * H)
    for half in range(2):
        gather_step(half, 2, 1, 0, 2 * H)
        gather_step(half, 3, 3, 0, 0)

    weight = jnp.where(lab_ref[...] == 1, LABEL, 1.0)

    @pl.loop(0, 8)
    def _(t):
        at = rows(t, R)
        place = lax.broadcasted_iota(jnp.int32, (R, E), 0) + t * R
        one = jnp.where(place == src_ref[...], 1.0, 0.0)
        two = jnp.where(place == dst_ref[...], 1.0, 0.0)
        both = one + two
        heavy = both * weight
        st[at, :] = both.astype(BF)
        wt[at, :] = heavy.astype(BF)
        cdeg[at, :] = jnp.broadcast_to(jnp.sum(one, axis=1, keepdims=True), (R, R))
        selfw[at, :] = jnp.broadcast_to(jnp.sum(one * two * weight, axis=1, keepdims=True), (R, R))

    def pair_counts(t):
        at = rows(t, 256)
        full = nt(st[at, :], wt[...])
        ones = jnp.floor(full * (1.0 / LABEL))
        many = full * 0.5 - (0.5 * LABEL - 0.5) * ones
        cnt[at, :] = many
        off[at, :] = many - ones
        alone = selfw[at, :1]
        ones = jnp.floor(alone * (1.0 / LABEL))
        many = alone - (LABEL - 1.0) * ones
        same = lax.broadcasted_iota(jnp.int32, (256, 256), 0) == lax.broadcasted_iota(jnp.int32, (256, 256), 1)
        cnt[at, at] = jnp.where(same, many, cnt[at, at])
        off[at, at] = jnp.where(same, many - 2.0 * ones, off[at, at])

    pl.loop(0, 2)(pair_counts)

    for half in range(2):
        ag2[half, 0].wait_recv()
        gather_step(half, 4, 1, 3, 0)
        ag2[half, 1].wait_recv()
        gather_step(half, 5, 3, 1, 2 * H)

    pl.loop(2, 4)(pair_counts)

    for half in range(2):
        for k in range(2, 6):
            ag2[half, k].wait_recv()
    for dx in (0, 2, 3, 1):
        for dc in range(2):
            if (dx, dc) != (0, 0):
                slot_cp[DOM.index((dx, dc))].wait_recv()
        at = rows(plus(x, 4 - dx), 256)
        cslots[at, :] = (slots[at, :].astype(F32) * (cdeg[at, :1] * (1.0 / 32))).astype(BF)
        dneg = (jnp.tanh(nt(slots[at, :], cand[...])) + 1.0).astype(BF)
        gneg[at, :] = nn(dneg, cand[...])
        dnt[:, at] = jnp.transpose(dneg)

    ret_cp = []
    rs_cp = {}

    def slot_grads(dx):
        at = rows(plus(x, dx), 256)
        pos = nt(slots[at, :] * jnp.asarray(0.5, BF), slots[...])
        w = (cnt[at, :] * jnp.tanh(pos) + off[at, :]).astype(BF)
        gst[at, :] = (gneg[at, :] * (cdeg[at, :1] * (1.0 / 16)) + nn(w, slots[...])).astype(BF)
        for dc in range(2):
            if (dx, dc) == (0, 0):
                cp = pltpu.make_async_copy(gst.at[rows(d, R)], ret.at[rows(d, R)], own_sem)
                cp.start()
                own_cp.append(cp)
                continue
            i = DOM.index((dx, dc))
            peer = dom_peer(dx, dc)
            cp = remote(gst.at[rows(peer, R)], ret.at[rows(d, R)], s_ret.at[i], r_ret.at[i], (e, peer))
            cp.start()
            ret_cp.append(cp)

    own_cp = []

    def reduce_step(half, k, src, dst, to):
        cp = remote(src, dst, s_rs1.at[half * 6 + k], r_rs1.at[half * 6 + k], across(half, to))
        cp.start()
        rs_cp[half, k] = cp

    lo, hi = pl.ds(0, 2 * H), pl.ds(2 * H, 2 * H)
    sides = ((1, lo, hi, 0), (3, hi, lo, 1))

    for half in range(2):
        opp[half] = nn(dnt[group(half, 2), :], cslots[...]).astype(BF)
        reduce_step(half, 0, opp.at[half, lo], rly.at[half * 2], 1)
        reduce_step(half, 1, opp.at[half, hi], rly.at[half * 2 + 1], 3)
    slot_grads(2)
    for half in range(2):
        for by, late, early, s in sides:
            n = half * 2 + s
            total = nn(dnt[group(half, by), :], cslots[...])
            side[n] = total.astype(BF)
            kept[n] = total[2 * H * s : 2 * H * (s + 1), :]
            reduce_step(half, 2 + s, side.at[n, early], rs1.at[n, early], by)
    slot_grads(1)
    slot_grads(3)
    for half in range(2):
        for by, late, early, s in sides:
            n = half * 2 + s
            rs_cp[half, s].wait_recv()
            side[n, late, :] = (kept[n] + rly[n].astype(F32)).astype(BF)
            reduce_step(half, 4 + s, side.at[n, late], rs1.at[n, late], by)
    for half in range(2):
        gcown[half] = nn(dnt[group(half, 0), :], cslots[...])
    slot_grads(0)

    for half in range(2):
        for k in range(2, 6):
            rs_cp[half, k].wait_recv()
    rs2_cp = []
    for half in range(2):
        part[half] = gcown[half] + rs1[half * 2].astype(F32) + rs1[half * 2 + 1].astype(F32)
        for i, by in enumerate(RING):
            k = half * 3 + i
            cp = remote(
                part.at[half, rows(plus(inner[half], by), H)], rs2.at[k], s_rs2.at[k], r_rs2.at[k], along(half, by)
            )
            cp.start()
            rs2_cp.append(cp)
    asked_out[...] = asked[...]
    for cp in ret_cp:
        cp.wait_recv()
    for cp in rs2_cp:
        cp.wait_recv()
    for half in range(2):
        total = part[half, rows(inner[half], H), :]
        for i in range(3):
            total = total + rs2[half * 3 + i]
        neg_out[half * H : (half + 1) * H, :] = total

    own_cp[0].wait()
    for cp in req_cp + ag1 + list(ag2.values()) + slot_cp + ret_cp + list(rs_cp.values()) + rs2_cp:
        cp.wait_send()


def scatter_kernel(ret, asked, neg_ref, neg, out_ref):
    base = pl.program_id(0) * 256
    hot = jnp.concatenate([onehot_columns(asked[p, :1, :], 256, base) for p in range(8)], axis=1)
    cols = onehot_columns(neg_ref[...], 256, base)
    high = neg[...].astype(BF)
    low = (neg[...] - high.astype(F32)).astype(BF)
    out_ref[...] = nn(hot, ret[...]) + nn(cols, high) + nn(cols, low)


def local(table, requests, edge_src, edge_dst, labels, neg_ids):
    vmem = pl.BlockSpec(memory_space=pltpu.VMEM)
    hbm = pl.BlockSpec(memory_space=pl.ANY)
    dma = pltpu.SemaphoreType.DMA
    negs = neg_ids.reshape(1, R)
    ret, asked, neg = pl.pallas_call(
        step_kernel,
        out_shape=(
            jax.ShapeDtypeStruct((S, D), BF),
            jax.ShapeDtypeStruct((8, 8, R), jnp.int32),
            jax.ShapeDtypeStruct((R, D), F32),
        ),
        in_specs=[hbm] + [vmem] * 5,
        out_specs=(hbm, vmem, vmem),
        scratch_shapes=[
            pltpu.VMEM((V, D), BF),
            pltpu.VMEM((8, 8, R), jnp.int32),
            pltpu.VMEM((8, 8, R), jnp.int32),
            pltpu.VMEM((S, D), BF),
            pltpu.VMEM((S, D), BF),
            pltpu.VMEM((S, D), BF),
            pltpu.VMEM((C, D), BF),
            pltpu.VMEM((C, S), BF),
            pltpu.VMEM((S, E), BF),
            pltpu.VMEM((S, E), BF),
            pltpu.VMEM((S, S), F32),
            pltpu.VMEM((S, S), F32),
            pltpu.VMEM((S, R), F32),
            pltpu.VMEM((S, R), F32),
            pltpu.VMEM((S, D), F32),
            pltpu.VMEM((S, D), BF),
            pltpu.VMEM((2, 4 * H, D), BF),
            pltpu.VMEM((4, 4 * H, D), BF),
            pltpu.VMEM((4, 2 * H, D), F32),
            pltpu.VMEM((2, 4 * H, D), F32),
            pltpu.VMEM((4, 2 * H, D), BF),
            pltpu.VMEM((4, 4 * H, D), BF),
            pltpu.VMEM((2, 4 * H, D), F32),
            pltpu.VMEM((6, H, D), F32),
            dma, dma,
            dma((7,)), dma((7,)),
            dma((7,)), dma((7,)),
            dma((6,)), dma((6,)),
            dma((12,)), dma((12,)),
            dma((7,)), dma((7,)),
            dma((12,)), dma((12,)),
            dma((6,)), dma((6,)),
        ],
        compiler_params=pltpu.CompilerParams(
            collective_id=0, has_side_effects=True, vmem_limit_bytes=56 * 1024 * 1024
        ),
        name="link_step",
    )(
        table,
        requests.reshape(8, R),
        edge_src.reshape(1, E),
        edge_dst.reshape(1, E),
        labels.reshape(1, E),
        negs,
    )
    whole = lambda shape: pl.BlockSpec(shape, lambda i: (0,) * len(shape))
    return pl.pallas_call(
        scatter_kernel,
        grid=(V // 256,),
        out_shape=jax.ShapeDtypeStruct((V, D), F32),
        in_specs=[whole((S, D)), whole((8, 8, R)), whole((1, R)), whole((R, D))],
        out_specs=pl.BlockSpec((256, D), lambda i: (i, 0)),
        compiler_params=pltpu.CompilerParams(vmem_limit_bytes=24 * 1024 * 1024),
        name="scatter",
    )(ret, asked, negs, neg)


def solution(mesh):
    return jax.shard_map(
        local,
        mesh=mesh,
        in_specs=(
            P(("eblock", "dom"), None),
            P("eblock", "dom", None, None),
            P("eblock", "dom", None),
            P("eblock", "dom", None),
            P("eblock", "dom", None),
            P("eblock", "dom", None),
        ),
        out_specs=P(("eblock", "dom"), None),
        check_vma=False,
    )
```

```python
import jax
import jax.numpy as jnp
from jax import lax
from jax.experimental import pallas as pl
from jax.experimental.pallas import tpu as pltpu
from jax.sharding import PartitionSpec as P

MESH = pl.DeviceIdType.MESH
BF = jnp.bfloat16
F32 = jnp.float32
D = 512
R = 128
S = 1024
E = 2048
C = 2048
V = 1024
H = 64
G = 4 * H
LABEL = 4096.0

DOM = ((1, 0), (1, 1), (3, 0), (3, 1), (2, 0), (2, 1), (0, 1))
RING = (2, 1, 3)
ORDER = (0, 1, 3, 2)


def nt(a, b):
    return lax.dot_general(a, b, (((1,), (1,)), ((), ())), preferred_element_type=F32)


def nn(a, b):
    return jnp.dot(a, b, preferred_element_type=F32)


def onehot_rows(ids, count):
    column = jnp.transpose(ids)[:, :1]
    return jnp.where(lax.broadcasted_iota(jnp.int32, (R, count), 1) == column, 1.0, 0.0).astype(BF)


def onehot_columns(ids, count, base=0):
    place = lax.broadcasted_iota(jnp.int32, (count, ids.shape[1]), 0) + base
    return jnp.where(place == ids, 1.0, 0.0).astype(BF)


def rows(i, n):
    return pl.ds(pl.multiple_of(i * n, n), n)


def chunk(dx, dc):
    return pl.ds((dx * 2 + dc) * R, R)


def pair(dx):
    return pl.ds(dx * 2 * R, 2 * R)


def group(half, by, first=0, count=G):
    return pl.ds((ORDER.index(by) * 2 + half) * G + first, count)


def step_kernel(
    table_hbm, req_hbm, src_hbm, dst_hbm, lab_hbm, neg_hbm, ret, asked_out, rs2, part_out,
    table, req, src, dst, lab, neg, reqst, asked, picked, slots, cslots, cand, dnt, st, wt, cnt, off, cdeg, selfw,
    gneg, gst, opp, side, kept, gcown, rly, rs1, part, part_bf,
    in_sem, out_sem, s_req, r_req, s_slot, r_slot, s_ag1, r_ag1, s_ag2, r_ag2, s_ret, r_ret, s_rs1, r_rs1, s_rs2, r_rs2,
):
    e = lax.axis_index("eblock")
    d = lax.axis_index("dom")
    z, y = lax.div(e, 4), lax.rem(e, 4)
    x, c = lax.div(d, 2), lax.rem(d, 2)

    def plus(a, by, n=4):
        return lax.rem(a + by, n)

    def dom_peer(dx, dc):
        return plus(x, dx) * 2 + plus(c, dc, 2)

    def along(half, by):
        if half == 0:
            return (z * 4 + plus(y, by), d)
        return (plus(z, by) * 4 + y, d)

    def across(half, by):
        return along(1 - half, by)

    def remote(src, dst, ssem, rsem, to):
        return pltpu.make_async_remote_copy(
            src_ref=src, dst_ref=dst, send_sem=ssem, recv_sem=rsem, device_id=to, device_id_type=MESH
        )

    def local_copy(src, dst, sem):
        cp = pltpu.make_async_copy(src, dst, sem)
        cp.start()
        return cp

    barrier = pltpu.get_barrier_semaphore()
    for dx, dc in ((2, 0), (2, 1), (1, 0), (1, 1), (3, 0), (3, 1), (0, 1)):
        pl.semaphore_signal(barrier, inc=1, device_id=(e, dom_peer(dx, dc)), device_id_type=MESH)
    for by in RING:
        for half in range(2):
            pl.semaphore_signal(barrier, inc=1, device_id=along(half, by), device_id_type=MESH)

    loads = [
        local_copy(a, b, in_sem.at[i])
        for i, (a, b) in enumerate(
            ((req_hbm, req), (neg_hbm, neg), (table_hbm, table), (src_hbm, src), (dst_hbm, dst), (lab_hbm, lab))
        )
    ]
    loads[0].wait()
    for p in range(8):
        reqst[p] = jnp.broadcast_to(req[p : p + 1, :], (8, R))
    loads[1].wait()
    neg_hot = onehot_rows(jnp.broadcast_to(neg[...], (8, R)), V)
    pl.semaphore_wait(barrier, 13)

    req_cp = {}
    for i, (dx, dc) in enumerate(((2, 0), (2, 1), (1, 0), (1, 1), (3, 0), (3, 1), (0, 1))):
        peer = dom_peer(dx, dc)
        cp = remote(reqst.at[peer], asked.at[(4 - dx) % 4 * 2 + dc], s_req.at[i], r_req.at[i], (e, peer))
        cp.start()
        req_cp[dx, dc] = cp
    asked[0] = reqst[d]

    loads[2].wait()
    own = (nn(neg_hot, table[...]) * 0.5).astype(BF)
    ag1 = {}
    ag2 = {}

    def gather_step(half, k, to, by, first, count):
        cp = remote(
            cand.at[group(half, by, first, count)], cand.at[group(half, (by - to) % 4, first, count)],
            s_ag2.at[half * 10 + k], r_ag2.at[half * 10 + k], across(half, to),
        )
        cp.start()
        ag2[half, k] = cp

    for half in range(2):
        cand[group(half, 0, 0, H), :] = own[half * H : (half + 1) * H, :]
    for by in RING:
        for half in range(2):
            k = half * 3 + RING.index(by)
            place = group(half, 0, ORDER.index((4 - by) % 4) * H, H)
            cp = remote(cand.at[group(half, 0, 0, H)], cand.at[place], s_ag1.at[k], r_ag1.at[k], along(half, by))
            cp.start()
            ag1[half, by] = cp
    for half in range(2):
        gather_step(half, 0, 1, 0, 0, H)
        gather_step(half, 1, 3, 0, 0, H)

    for cp in loads[3:]:
        cp.wait()
    weight = jnp.where(lab[...] == 1, LABEL, 1.0)

    @pl.loop(0, 8)
    def _(t):
        at = rows(t, R)
        first = dom_peer(lax.div(t, 2), lax.rem(t, 2)) * R
        place = lax.broadcasted_iota(jnp.int32, (R, E), 0) + first
        one = jnp.where(place == src[...], 1.0, 0.0)
        two = jnp.where(place == dst[...], 1.0, 0.0)
        both = one + two
        st[at, :] = both.astype(BF)
        wt[at, :] = (both * weight).astype(BF)
        cdeg[at, :] = jnp.broadcast_to(jnp.sum(one, axis=1, keepdims=True), (R, R))
        selfw[at, :] = jnp.broadcast_to(jnp.sum(one * two * weight, axis=1, keepdims=True), (R, R))

    for cp in req_cp.values():
        cp.wait_recv()
    slot_cp = {}
    for dx in (1, 3, 2, 0):
        hot = jnp.concatenate([onehot_rows(asked[dx * 2], V), onehot_rows(asked[dx * 2 + 1], V)], axis=0)
        rows_out = nn(hot, table[...]).astype(BF)
        if dx == 0:
            slots[chunk(0, 0), :] = rows_out[:R, :]
            picked[chunk(0, 1), :] = rows_out[R:, :]
        else:
            picked[pair(dx), :] = rows_out
        for dc in range(2):
            if (dx, dc) == (0, 0):
                continue
            i = DOM.index((dx, dc))
            cp = remote(
                picked.at[chunk(dx, dc)], slots.at[chunk((4 - dx) % 4, dc)],
                s_slot.at[i], r_slot.at[i], (e, dom_peer(dx, dc)),
            )
            cp.start()
            slot_cp[dx, dc] = cp
    asked_cp = local_copy(asked, asked_out, out_sem.at[0])

    for cp in ag1.values():
        cp.wait_recv()
    for half in range(2):
        gather_step(half, 2, 1, 0, H, 96)
        gather_step(half, 3, 3, 0, H + 96, 96)
    for half in range(2):
        gather_step(half, 4, 1, 0, H + 96, 96)
        gather_step(half, 5, 3, 0, H, 96)
    for half in range(2):
        ag2[half, 0].wait_recv()
        gather_step(half, 6, 1, 3, 0, H // 2)
        ag2[half, 1].wait_recv()
        gather_step(half, 7, 3, 1, H // 2, H // 2)

    def pair_counts(t):
        at = rows(t, 256)
        full = nt(st[at, :], wt[...])
        ones = jnp.floor(full * (1.0 / LABEL))
        many = full * 0.5 - (0.5 * LABEL - 0.5) * ones
        cnt[at, :] = many
        off[at, :] = many - ones
        alone = selfw[at, :1]
        ones = jnp.floor(alone * (1.0 / LABEL))
        many = alone - (LABEL - 1.0) * ones
        same = lax.broadcasted_iota(jnp.int32, (256, 256), 0) == lax.broadcasted_iota(jnp.int32, (256, 256), 1)
        cnt[at, at] = jnp.where(same, many, cnt[at, at])
        off[at, at] = jnp.where(same, many - 2.0 * ones, off[at, at])

    pl.loop(0, 3)(pair_counts)

    for half in range(2):
        ag2[half, 2].wait_recv()
        gather_step(half, 8, 1, 3, H, 96)
        ag2[half, 3].wait_recv()
        gather_step(half, 9, 3, 1, H + 96, 96)

    pl.loop(3, 4)(pair_counts)

    for half in range(2):
        for k in range(4, 10):
            ag2[half, k].wait_recv()
    lost = jnp.zeros((1, D), F32)
    for dx in (0, 1, 3, 2):
        for dc in range(2):
            if (dx, dc) != (0, 0):
                slot_cp[(4 - dx) % 4, dc].wait_recv()
        at = pair(dx)
        many = slots[at, :].astype(F32) * (cdeg[at, :1] * (1.0 / 32))
        kept_many = many.astype(BF)
        cslots[at, :] = kept_many
        lost = lost + jnp.sum(many - kept_many.astype(F32), axis=0, keepdims=True)
        dneg = (jnp.tanh(nt(slots[at, :], cand[...])) + 1.0).astype(BF)
        gneg[at, :] = nn(dneg, cand[...])
        dnt[:, at] = jnp.transpose(dneg)

    ret_cp = []
    rs_cp = {}

    def slot_grads(dx):
        at = pair(dx)
        pos = nt(slots[at, :] * jnp.asarray(0.5, BF), slots[...])
        w = (cnt[at, :] * jnp.tanh(pos) + off[at, :]).astype(BF)
        gst[at, :] = (gneg[at, :] * (cdeg[at, :1] * (1.0 / 16)) + nn(w, slots[...])).astype(BF)
        for dc in range(2):
            if (dx, dc) == (0, 0):
                continue
            i = DOM.index((dx, dc))
            cp = remote(
                gst.at[chunk(dx, dc)], ret.at[chunk((4 - dx) % 4, dc)],
                s_ret.at[i], r_ret.at[i], (e, dom_peer(dx, dc)),
            )
            cp.start()
            ret_cp.append(cp)

    def cand_grads(half, by):
        return nn(dnt[group(half, by), :], cslots[...]) + lost

    def reduce_step(half, k, src, dst, to):
        cp = remote(src, dst, s_rs1.at[half * 6 + k], r_rs1.at[half * 6 + k], across(half, to))
        cp.start()
        rs_cp[half, k] = cp

    lo, hi = pl.ds(0, 2 * H), pl.ds(2 * H, 2 * H)
    sides = ((1, lo, hi, 0), (3, hi, lo, 1))

    def opposite(half):
        opp[half] = cand_grads(half, 2).astype(BF)
        reduce_step(half, 0, opp.at[half, lo], rly.at[half * 2], 1)
        reduce_step(half, 1, opp.at[half, hi], rly.at[half * 2 + 1], 3)

    def neighbours_early(half):
        for by, late, early, s in sides:
            n = half * 2 + s
            total = cand_grads(half, by)
            side[n] = total.astype(BF)
            kept[n] = total[2 * H * s : 2 * H * (s + 1), :]
            reduce_step(half, 2 + s, side.at[n, early], rs1.at[n, early], by)

    def neighbours_late(half):
        for by, late, early, s in sides:
            n = half * 2 + s
            rs_cp[half, s].wait_recv()
            side[n, late, :] = (kept[n] + rly[n].astype(F32)).astype(BF)
            reduce_step(half, 4 + s, side.at[n, late], rs1.at[n, late], by)

    def own_group(half):
        gcown[half] = cand_grads(half, 0)

    opposite(0)
    opposite(1)
    slot_grads(1)
    neighbours_early(0)
    neighbours_early(1)
    slot_grads(3)
    slot_grads(2)
    neighbours_late(0)
    neighbours_late(1)
    own_group(0)
    own_group(1)
    slot_grads(0)
    own_cp = local_copy(gst.at[chunk(0, 0)], ret.at[chunk(0, 0)], out_sem.at[1])

    rs2_cp = []
    for half in range(2):
        for k in range(2, 6):
            rs_cp[half, k].wait_recv()
        total = gcown[half] + rs1[half * 2].astype(F32) + rs1[half * 2 + 1].astype(F32)
        part[half] = total[:H, :]
        part_bf[half] = total.astype(BF)
        for by in RING:
            k = half * 3 + RING.index(by)
            cp = remote(
                part_bf.at[half, pl.ds(ORDER.index(by) * H, H)], rs2.at[pl.ds(k * H, H)],
                s_rs2.at[k], r_rs2.at[k], along(half, by),
            )
            cp.start()
            rs2_cp.append(cp)
    part_cp = local_copy(part, part_out, out_sem.at[2])
    for cp in ret_cp:
        cp.wait_recv()
    for cp in rs2_cp:
        cp.wait_recv()

    for cp in (asked_cp, own_cp, part_cp):
        cp.wait()
    for cps in (req_cp, ag1, ag2, slot_cp, rs_cp):
        for cp in cps.values():
            cp.wait_send()
    for cp in ret_cp + rs2_cp:
        cp.wait_send()


def scatter_kernel(
    ret_hbm, asked_hbm, neg_hbm, rs2_hbm, part_hbm, out_hbm, ret, asked, neg, rs2, part, out, in_sem, out_sem
):
    pairs = ((asked_hbm, asked), (ret_hbm, ret.at[pl.ds(0, S)]), (neg_hbm, neg), (rs2_hbm, rs2), (part_hbm, part))
    loads = []
    for i, (a, b) in enumerate(pairs):
        cp = pltpu.make_async_copy(a, b, in_sem.at[i])
        cp.start()
        loads.append(cp)
    loads[0].wait()
    loads[2].wait()
    hots = []
    for t in range(4):
        hots.append(
            jnp.concatenate(
                [onehot_columns(asked[p, :1, :], 256, t * 256) for p in range(8)]
                + [onehot_columns(neg[...], 256, t * 256)] * 2,
                axis=1,
            )
        )
    loads[3].wait()
    loads[4].wait()
    for half in range(2):
        total = part[half]
        for i in range(3):
            k = half * 3 + i
            total = total + rs2[k * H : (k + 1) * H, :].astype(F32)
        high = total.astype(BF)
        ret[S + half * H : S + (half + 1) * H, :] = high
        ret[S + R + half * H : S + R + (half + 1) * H, :] = (total - high.astype(F32)).astype(BF)
    loads[1].wait()
    stores = []
    for t in range(4):
        at = pl.ds(t * 256, 256)
        out[at, :] = nn(hots[t], ret[...])
        cp = pltpu.make_async_copy(out.at[at], out_hbm.at[at], out_sem.at[t])
        cp.start()
        stores.append(cp)
    for cp in stores:
        cp.wait()


def local(table, requests, edge_src, edge_dst, labels, neg_ids):
    hbm = pl.BlockSpec(memory_space=pltpu.HBM)
    dma = pltpu.SemaphoreType.DMA
    negs = neg_ids.reshape(1, R)
    ids = pltpu.VMEM((1, E), jnp.int32)
    ret, asked, rs2, part = pl.pallas_call(
        step_kernel,
        out_shape=(
            jax.ShapeDtypeStruct((S, D), BF),
            jax.ShapeDtypeStruct((8, 8, R), jnp.int32),
            jax.ShapeDtypeStruct((6 * H, D), BF),
            jax.ShapeDtypeStruct((2, H, D), F32),
        ),
        in_specs=[hbm] * 6,
        out_specs=(hbm,) * 4,
        scratch_shapes=[
            pltpu.VMEM((V, D), BF),
            pltpu.VMEM((8, R), jnp.int32),
            ids, ids, ids,
            pltpu.VMEM((1, R), jnp.int32),
            pltpu.VMEM((8, 8, R), jnp.int32),
            pltpu.VMEM((8, 8, R), jnp.int32),
            pltpu.VMEM((S, D), BF),
            pltpu.VMEM((S, D), BF),
            pltpu.VMEM((S, D), BF),
            pltpu.VMEM((C, D), BF),
            pltpu.VMEM((C, S), BF),
            pltpu.VMEM((S, E), BF),
            pltpu.VMEM((S, E), BF),
            pltpu.VMEM((S, S), F32),
            pltpu.VMEM((S, S), F32),
            pltpu.VMEM((S, R), F32),
            pltpu.VMEM((S, R), F32),
            pltpu.VMEM((S, D), F32),
            pltpu.VMEM((S, D), BF),
            pltpu.VMEM((2, G, D), BF),
            pltpu.VMEM((4, G, D), BF),
            pltpu.VMEM((4, 2 * H, D), F32),
            pltpu.VMEM((2, G, D), F32),
            pltpu.VMEM((4, 2 * H, D), BF),
            pltpu.VMEM((4, G, D), BF),
            pltpu.VMEM((2, H, D), F32),
            pltpu.VMEM((2, G, D), BF),
            dma((6,)), dma((3,)),
            dma((7,)), dma((7,)),
            dma((7,)), dma((7,)),
            dma((6,)), dma((6,)),
            dma((20,)), dma((20,)),
            dma((7,)), dma((7,)),
            dma((12,)), dma((12,)),
            dma((6,)), dma((6,)),
        ],
        compiler_params=pltpu.CompilerParams(
            collective_id=0, has_side_effects=True, vmem_limit_bytes=56 * 1024 * 1024
        ),
        name="link_step",
    )(
        table,
        requests.reshape(8, R),
        edge_src.reshape(1, E),
        edge_dst.reshape(1, E),
        labels.reshape(1, E),
        negs,
    )
    return pl.pallas_call(
        scatter_kernel,
        out_shape=jax.ShapeDtypeStruct((V, D), F32),
        in_specs=[hbm] * 5,
        out_specs=hbm,
        scratch_shapes=[
            pltpu.VMEM((S + 2 * R, D), BF),
            pltpu.VMEM((8, 8, R), jnp.int32),
            pltpu.VMEM((1, R), jnp.int32),
            pltpu.VMEM((6 * H, D), BF),
            pltpu.VMEM((2, H, D), F32),
            pltpu.VMEM((V, D), F32),
            dma((5,)), dma((4,)),
        ],
        compiler_params=pltpu.CompilerParams(vmem_limit_bytes=56 * 1024 * 1024),
        name="scatter",
    )(ret, asked, negs, rs2, part)


def solution(mesh):
    return jax.shard_map(
        local,
        mesh=mesh,
        in_specs=(
            P(("eblock", "dom"), None),
            P("eblock", "dom", None, None),
            P("eblock", "dom", None),
            P("eblock", "dom", None),
            P("eblock", "dom", None),
            P("eblock", "dom", None),
        ),
        out_specs=P(("eblock", "dom"), None),
        check_vma=False,
    )
```

```python
import jax
import jax.numpy as jnp
from jax import lax
from jax.experimental import pallas as pl
from jax.experimental.pallas import tpu as pltpu
from jax.sharding import PartitionSpec as P

MESH = pl.DeviceIdType.MESH
BF = jnp.bfloat16
F32 = jnp.float32
D = 512
R = 128
S = 1024
E = 2048
C = 2048
V = 1024
H = 64
G = 4 * H
LABEL = 4096.0

DOM = ((1, 0), (1, 1), (3, 0), (3, 1), (2, 0), (2, 1), (0, 1))
RING = (2, 1, 3)
ORDER = (0, 1, 3, 2)


def nt(a, b):
    return lax.dot_general(a, b, (((1,), (1,)), ((), ())), preferred_element_type=F32)


def nn(a, b):
    return jnp.dot(a, b, preferred_element_type=F32)


def onehot_rows(ids, count):
    column = jnp.transpose(ids)[:, :1]
    return jnp.where(lax.broadcasted_iota(jnp.int32, (R, count), 1) == column, 1.0, 0.0).astype(BF)


def onehot_columns(ids, count, base=0):
    place = lax.broadcasted_iota(jnp.int32, (count, ids.shape[1]), 0) + base
    return jnp.where(place == ids, 1.0, 0.0).astype(BF)


def rows(i, n):
    return pl.ds(pl.multiple_of(i * n, n), n)


def chunk(dx, dc):
    return pl.ds((dx * 2 + dc) * R, R)


def pair(dx):
    return pl.ds(dx * 2 * R, 2 * R)


def group(half, by, first=0, count=G):
    return pl.ds((ORDER.index(by) * 2 + half) * G + first, count)


def step_kernel(
    table_hbm, req_hbm, src_hbm, dst_hbm, lab_hbm, neg_hbm, ret, asked_out, rs2, part_out,
    table, req, src, dst, lab, neg, reqst, asked, picked, slots, cslots, cand, dnt, st, wt, cnt, off, cdeg,
    gneg, gst, opp, side, kept, gcown, rly, rs1, part, part_bf,
    in_sem, out_sem, s_req, r_req, s_slot, r_slot, s_ag1, r_ag1, s_ag2, r_ag2, s_ret, r_ret, s_rs1, r_rs1, s_rs2, r_rs2,
):
    e = lax.axis_index("eblock")
    d = lax.axis_index("dom")
    z, y = lax.div(e, 4), lax.rem(e, 4)
    x, c = lax.div(d, 2), lax.rem(d, 2)

    def plus(a, by, n=4):
        return lax.rem(a + by, n)

    def dom_peer(dx, dc):
        return plus(x, dx) * 2 + plus(c, dc, 2)

    def along(half, by):
        if half == 0:
            return (z * 4 + plus(y, by), d)
        return (plus(z, by) * 4 + y, d)

    def across(half, by):
        return along(1 - half, by)

    def remote(src, dst, ssem, rsem, to):
        return pltpu.make_async_remote_copy(
            src_ref=src, dst_ref=dst, send_sem=ssem, recv_sem=rsem, device_id=to, device_id_type=MESH
        )

    def local_copy(src, dst, sem):
        cp = pltpu.make_async_copy(src, dst, sem)
        cp.start()
        return cp

    barrier = pltpu.get_barrier_semaphore()
    for dx, dc in ((2, 0), (2, 1), (1, 0), (1, 1), (3, 0), (3, 1), (0, 1)):
        pl.semaphore_signal(barrier, inc=1, device_id=(e, dom_peer(dx, dc)), device_id_type=MESH)
    for by in RING:
        for half in range(2):
            pl.semaphore_signal(barrier, inc=1, device_id=along(half, by), device_id_type=MESH)

    loads = [
        local_copy(a, b, in_sem.at[i])
        for i, (a, b) in enumerate(
            ((req_hbm, req), (neg_hbm, neg), (table_hbm, table), (src_hbm, src), (dst_hbm, dst), (lab_hbm, lab))
        )
    ]
    loads[0].wait()
    for p in range(8):
        reqst[p] = jnp.broadcast_to(req[p : p + 1, :], (8, R))
    loads[1].wait()
    neg_hot = onehot_rows(jnp.broadcast_to(neg[...], (8, R)), V)
    pl.semaphore_wait(barrier, 13)

    req_cp = {}
    for i, (dx, dc) in enumerate(((2, 0), (2, 1), (1, 0), (1, 1), (3, 0), (3, 1), (0, 1))):
        peer = dom_peer(dx, dc)
        cp = remote(reqst.at[peer], asked.at[(4 - dx) % 4 * 2 + dc], s_req.at[i], r_req.at[i], (e, peer))
        cp.start()
        req_cp[dx, dc] = cp
    asked[0] = reqst[d]

    loads[2].wait()
    own = (nn(neg_hot, table[...]) * 0.5).astype(BF)
    ag1 = {}
    ag2 = {}

    def gather_step(half, k, to, by, first, count):
        cp = remote(
            cand.at[group(half, by, first, count)], cand.at[group(half, (by - to) % 4, first, count)],
            s_ag2.at[half * 14 + k], r_ag2.at[half * 14 + k], across(half, to),
        )
        cp.start()
        ag2[half, k] = cp

    for half in range(2):
        cand[group(half, 0, 0, H), :] = own[half * H : (half + 1) * H, :]
    def short_step(by):
        for half in range(2):
            k = half * 3 + RING.index(by)
            place = group(half, 0, ORDER.index((4 - by) % 4) * H, H)
            cp = remote(cand.at[group(half, 0, 0, H)], cand.at[place], s_ag1.at[k], r_ag1.at[k], along(half, by))
            cp.start()
            ag1[half, by] = cp

    short_step(1)
    short_step(3)
    for half in range(2):
        gather_step(half, 0, 1, 0, 0, H)
        gather_step(half, 1, 3, 0, 0, H)
    short_step(2)

    for cp in loads[3:]:
        cp.wait()
    weight = jnp.where(lab[...] == 1, LABEL, 1.0)
    line = lax.broadcasted_iota(jnp.int32, (R, E), 0)
    loop_weight = jnp.where(src[...] == dst[...], weight, 0.0)
    sums = jnp.where(line == 0, 1.0, jnp.where(line == 1, loop_weight, 0.0)).astype(BF)
    weight = weight.astype(BF)
    line = line.astype(F32).astype(BF)

    def incidence(t):
        at = rows(t, R)
        first = dom_peer(lax.div(t, 2), lax.rem(t, 2)) * R

        def ends(ids):
            place = ids[...] - first
            place = jnp.where((place >= 0) & (place < R), place, R).astype(F32).astype(BF)
            return jnp.where(line == place, jnp.ones((R, E), BF), jnp.zeros((R, E), BF))

        one = ends(src)
        both = one + ends(dst)
        st[at, :] = both.astype(BF)
        wt[at, :] = (both * weight).astype(BF)
        cdeg[at, :] = nt(one, sums)

    pl.loop(0, 4)(incidence)

    for cp in req_cp.values():
        cp.wait_recv()
    slot_cp = {}
    for dx in (1, 3, 2, 0):
        hot = jnp.concatenate([onehot_rows(asked[dx * 2], V), onehot_rows(asked[dx * 2 + 1], V)], axis=0)
        rows_out = nn(hot, table[...]).astype(BF)
        if dx == 0:
            slots[chunk(0, 0), :] = rows_out[:R, :]
            picked[chunk(0, 1), :] = rows_out[R:, :]
        else:
            picked[pair(dx), :] = rows_out
        for dc in range(2):
            if (dx, dc) == (0, 0):
                continue
            i = DOM.index((dx, dc))
            cp = remote(
                picked.at[chunk(dx, dc)], slots.at[chunk((4 - dx) % 4, dc)],
                s_slot.at[i], r_slot.at[i], (e, dom_peer(dx, dc)),
            )
            cp.start()
            slot_cp[dx, dc] = cp
    asked_cp = local_copy(asked, asked_out, out_sem.at[0])

    for half in range(2):
        for by in (1, 3):
            ag1[half, by].wait_recv()
    for half in range(2):
        gather_step(half, 2, 1, 0, H, H)
        gather_step(half, 3, 3, 0, 2 * H, H)
    for half in range(2):
        gather_step(half, 4, 1, 0, 2 * H, H)
        gather_step(half, 5, 3, 0, H, H)
    for half in range(2):
        ag2[half, 0].wait_recv()
        gather_step(half, 8, 1, 3, 0, H // 2)
        ag2[half, 1].wait_recv()
        gather_step(half, 9, 3, 1, H // 2, H // 2)
    pl.loop(4, 8)(incidence)
    for half in range(2):
        ag1[half, 2].wait_recv()
        gather_step(half, 6, 1, 0, 3 * H, H)
        gather_step(half, 7, 3, 0, 3 * H, H)

    def pair_counts(t):
        at = rows(t, 256)
        full = nt(st[at, :], wt[...])
        ones = jnp.floor(full * (1.0 / LABEL))
        many = full * 0.5 - (0.5 * LABEL - 0.5) * ones
        cnt[at, :] = many
        off[at, :] = many - ones
        alone = cdeg[at, 1:2]
        ones = jnp.floor(alone * (1.0 / LABEL))
        many = alone - (LABEL - 1.0) * ones
        same = lax.broadcasted_iota(jnp.int32, (256, 256), 0) == lax.broadcasted_iota(jnp.int32, (256, 256), 1)
        cnt[at, at] = jnp.where(same, many, cnt[at, at])
        off[at, at] = jnp.where(same, many - 2.0 * ones, off[at, at])

    pl.loop(0, 1)(pair_counts)

    for half in range(2):
        ag2[half, 2].wait_recv()
        gather_step(half, 10, 1, 3, H, H)
        ag2[half, 3].wait_recv()
        gather_step(half, 11, 3, 1, 2 * H, H)

    pl.loop(1, 3)(pair_counts)
    for half in range(2):
        ag2[half, 6].wait_recv()
        gather_step(half, 12, 1, 3, 3 * H, H // 2)
        ag2[half, 7].wait_recv()
        gather_step(half, 13, 3, 1, 3 * H + H // 2, H // 2)
    pl.loop(3, 4)(pair_counts)

    for half in range(2):
        for k in (4, 5):
            ag2[half, k].wait_recv()
    near, far = pl.ds(0, 6 * G), pl.ds(6 * G, 2 * G)
    lost = jnp.zeros((1, D), F32)

    def arrive(dx, lost):
        for dc in range(2):
            if (dx, dc) != (0, 0):
                slot_cp[(4 - dx) % 4, dc].wait_recv()
        at = pair(dx)
        many = slots[at, :].astype(F32) * (cdeg[at, :1] * (1.0 / 32))
        kept_many = many.astype(BF)
        cslots[at, :] = kept_many
        return lost + jnp.sum(many - kept_many.astype(F32), axis=0, keepdims=True)

    def score(dx, block, add):
        at = pair(dx)
        dneg = (jnp.tanh(nt(slots[at, :], cand[block, :])) + 1.0).astype(BF)
        more = nn(dneg, cand[block, :])
        gneg[at, :] = gneg[at, :] + more if add else more
        dnt[block, at] = jnp.transpose(dneg)

    for dx in (0, 1, 3, 2)[:3]:
        lost = arrive(dx, lost)
        score(dx, near, False)
    for half in range(2):
        for k in range(8, 14):
            ag2[half, k].wait_recv()
    for dx in (0, 1, 3, 2)[:3]:
        score(dx, far, True)
    lost = arrive((0, 1, 3, 2)[3], lost)
    score((0, 1, 3, 2)[3], pl.ds(0, C), False)

    ret_cp = []
    rs_cp = {}

    def slot_grads(dx):
        at = pair(dx)
        pos = nt(slots[at, :] * jnp.asarray(0.5, BF), slots[...])
        w = (cnt[at, :] * jnp.tanh(pos) + off[at, :]).astype(BF)
        gst[at, :] = (gneg[at, :] * (cdeg[at, :1] * (1.0 / 16)) + nn(w, slots[...])).astype(BF)
        for dc in range(2):
            if (dx, dc) == (0, 0):
                continue
            i = DOM.index((dx, dc))
            cp = remote(
                gst.at[chunk(dx, dc)], ret.at[chunk((4 - dx) % 4, dc)],
                s_ret.at[i], r_ret.at[i], (e, dom_peer(dx, dc)),
            )
            cp.start()
            ret_cp.append(cp)

    def cand_grads(half, by):
        return nn(dnt[group(half, by), :], cslots[...]) + lost

    def reduce_step(half, k, src, dst, to):
        cp = remote(src, dst, s_rs1.at[half * 6 + k], r_rs1.at[half * 6 + k], across(half, to))
        cp.start()
        rs_cp[half, k] = cp

    lo, hi = pl.ds(0, 2 * H), pl.ds(2 * H, 2 * H)
    sides = ((1, lo, hi, 0), (3, hi, lo, 1))

    def opposite(half):
        opp[half] = cand_grads(half, 2).astype(BF)
        reduce_step(half, 0, opp.at[half, lo], rly.at[half * 2], 1)
        reduce_step(half, 1, opp.at[half, hi], rly.at[half * 2 + 1], 3)

    def neighbours_early(half):
        for by, late, early, s in sides:
            n = half * 2 + s
            total = cand_grads(half, by)
            side[n] = total.astype(BF)
            kept[n] = total[2 * H * s : 2 * H * (s + 1), :]
            reduce_step(half, 2 + s, side.at[n, early], rs1.at[n, early], by)

    def neighbours_late(half):
        for by, late, early, s in sides:
            n = half * 2 + s
            rs_cp[half, s].wait_recv()
            side[n, late, :] = (kept[n] + rly[n].astype(F32)).astype(BF)
            reduce_step(half, 4 + s, side.at[n, late], rs1.at[n, late], by)

    def own_group(half):
        gcown[half] = cand_grads(half, 0)

    opposite(0)
    opposite(1)
    slot_grads(2)
    neighbours_early(0)
    neighbours_early(1)
    slot_grads(1)
    slot_grads(3)
    neighbours_late(0)
    neighbours_late(1)
    own_group(0)
    own_group(1)
    slot_grads(0)
    own_cp = local_copy(gst.at[chunk(0, 0)], ret.at[chunk(0, 0)], out_sem.at[1])

    rs2_cp = []
    for half in range(2):
        for k in range(2, 6):
            rs_cp[half, k].wait_recv()
        total = gcown[half] + rs1[half * 2].astype(F32) + rs1[half * 2 + 1].astype(F32)
        part[half] = total[:H, :]
        part_bf[half] = total.astype(BF)
        for by in RING:
            k = half * 3 + RING.index(by)
            cp = remote(
                part_bf.at[half, pl.ds(ORDER.index(by) * H, H)], rs2.at[pl.ds(k * H, H)],
                s_rs2.at[k], r_rs2.at[k], along(half, by),
            )
            cp.start()
            rs2_cp.append(cp)
    part_cp = local_copy(part, part_out, out_sem.at[2])
    for cp in ret_cp:
        cp.wait_recv()
    for cp in rs2_cp:
        cp.wait_recv()

    for cp in (asked_cp, own_cp, part_cp):
        cp.wait()
    for cps in (req_cp, ag1, ag2, slot_cp, rs_cp):
        for cp in cps.values():
            cp.wait_send()
    for cp in ret_cp + rs2_cp:
        cp.wait_send()


def scatter_kernel(
    ret_hbm, asked_hbm, neg_hbm, rs2_hbm, part_hbm, out_hbm, ret, asked, neg, rs2, part, out, in_sem, out_sem
):
    pairs = ((asked_hbm, asked), (ret_hbm, ret.at[pl.ds(0, S)]), (neg_hbm, neg), (rs2_hbm, rs2), (part_hbm, part))
    loads = []
    for i, (a, b) in enumerate(pairs):
        cp = pltpu.make_async_copy(a, b, in_sem.at[i])
        cp.start()
        loads.append(cp)
    loads[0].wait()
    loads[2].wait()
    line = lax.broadcasted_iota(jnp.int32, (256, R), 0).astype(F32).astype(BF)

    def hot(ids, first):
        place = ids - first
        place = jnp.where((place >= 0) & (place < 256), place, 256).astype(F32).astype(BF)
        return jnp.where(line == place, jnp.ones((256, R), BF), jnp.zeros((256, R), BF))

    loads[3].wait()
    loads[4].wait()
    for half in range(2):
        total = part[half]
        for i in range(3):
            k = half * 3 + i
            total = total + rs2[k * H : (k + 1) * H, :].astype(F32)
        high = total.astype(BF)
        ret[S + half * H : S + (half + 1) * H, :] = high
        ret[S + R + half * H : S + R + (half + 1) * H, :] = (total - high.astype(F32)).astype(BF)
    loads[1].wait()
    stores = []
    for t in range(4):
        at = pl.ds(t * 256, 256)
        negs = hot(neg[...], t * 256)
        hots = jnp.concatenate([hot(asked[p, :1, :], t * 256) for p in range(8)] + [negs, negs], axis=1)
        out[at, :] = nn(hots, ret[...])
        cp = pltpu.make_async_copy(out.at[at], out_hbm.at[at], out_sem.at[t])
        cp.start()
        stores.append(cp)
    for cp in stores:
        cp.wait()


def local(table, requests, edge_src, edge_dst, labels, neg_ids):
    hbm = pl.BlockSpec(memory_space=pltpu.HBM)
    dma = pltpu.SemaphoreType.DMA
    negs = neg_ids.reshape(1, R)
    ids = pltpu.VMEM((1, E), jnp.int32)
    ret, asked, rs2, part = pl.pallas_call(
        step_kernel,
        out_shape=(
            jax.ShapeDtypeStruct((S, D), BF),
            jax.ShapeDtypeStruct((8, 8, R), jnp.int32),
            jax.ShapeDtypeStruct((6 * H, D), BF),
            jax.ShapeDtypeStruct((2, H, D), F32),
        ),
        in_specs=[hbm] * 6,
        out_specs=(hbm,) * 4,
        scratch_shapes=[
            pltpu.VMEM((V, D), BF),
            pltpu.VMEM((8, R), jnp.int32),
            ids, ids, ids,
            pltpu.VMEM((1, R), jnp.int32),
            pltpu.VMEM((8, 8, R), jnp.int32),
            pltpu.VMEM((8, 8, R), jnp.int32),
            pltpu.VMEM((S, D), BF),
            pltpu.VMEM((S, D), BF),
            pltpu.VMEM((S, D), BF),
            pltpu.VMEM((C, D), BF),
            pltpu.VMEM((C, S), BF),
            pltpu.VMEM((S, E), BF),
            pltpu.VMEM((S, E), BF),
            pltpu.VMEM((S, S), F32),
            pltpu.VMEM((S, S), F32),
            pltpu.VMEM((S, R), F32),
            pltpu.VMEM((S, D), F32),
            pltpu.VMEM((S, D), BF),
            pltpu.VMEM((2, G, D), BF),
            pltpu.VMEM((4, G, D), BF),
            pltpu.VMEM((4, 2 * H, D), F32),
            pltpu.VMEM((2, G, D), F32),
            pltpu.VMEM((4, 2 * H, D), BF),
            pltpu.VMEM((4, G, D), BF),
            pltpu.VMEM((2, H, D), F32),
            pltpu.VMEM((2, G, D), BF),
            dma((6,)), dma((3,)),
            dma((7,)), dma((7,)),
            dma((7,)), dma((7,)),
            dma((6,)), dma((6,)),
            dma((28,)), dma((28,)),
            dma((7,)), dma((7,)),
            dma((12,)), dma((12,)),
            dma((6,)), dma((6,)),
        ],
        compiler_params=pltpu.CompilerParams(
            collective_id=0, has_side_effects=True, vmem_limit_bytes=56 * 1024 * 1024
        ),
        name="link_step",
    )(
        table,
        requests.reshape(8, R),
        edge_src.reshape(1, E),
        edge_dst.reshape(1, E),
        labels.reshape(1, E),
        negs,
    )
    return pl.pallas_call(
        scatter_kernel,
        out_shape=jax.ShapeDtypeStruct((V, D), F32),
        in_specs=[hbm] * 5,
        out_specs=hbm,
        scratch_shapes=[
            pltpu.VMEM((S + 2 * R, D), BF),
            pltpu.VMEM((8, 8, R), jnp.int32),
            pltpu.VMEM((1, R), jnp.int32),
            pltpu.VMEM((6 * H, D), BF),
            pltpu.VMEM((2, H, D), F32),
            pltpu.VMEM((V, D), F32),
            dma((5,)), dma((4,)),
        ],
        compiler_params=pltpu.CompilerParams(vmem_limit_bytes=56 * 1024 * 1024),
        name="scatter",
    )(ret, asked, negs, rs2, part)


def solution(mesh):
    return jax.shard_map(
        local,
        mesh=mesh,
        in_specs=(
            P(("eblock", "dom"), None),
            P("eblock", "dom", None, None),
            P("eblock", "dom", None),
            P("eblock", "dom", None),
            P("eblock", "dom", None),
            P("eblock", "dom", None),
        ),
        out_specs=P(("eblock", "dom"), None),
        check_vma=False,
    )
```

```python
import jax
import jax.numpy as jnp
from jax import lax
from jax.experimental import pallas as pl
from jax.experimental.pallas import tpu as pltpu
from jax.sharding import PartitionSpec as P

MESH = pl.DeviceIdType.MESH
BF = jnp.bfloat16
F32 = jnp.float32
D = 512
R = 128
S = 1024
E = 2048
C = 2048
V = 1024
H = 64
G = 4 * H
LABEL = 4096.0

DOM = ((1, 0), (1, 1), (3, 0), (3, 1), (2, 0), (2, 1), (0, 1))
RING = (2, 1, 3)
ORDER = (0, 1, 3, 2)


def nt(a, b):
    return lax.dot_general(a, b, (((1,), (1,)), ((), ())), preferred_element_type=F32)


def nn(a, b):
    return jnp.dot(a, b, preferred_element_type=F32)


def onehot_rows(ids, count):
    column = jnp.transpose(ids)[:, :1]
    return jnp.where(lax.broadcasted_iota(jnp.int32, (R, count), 1) == column, 1.0, 0.0).astype(BF)


def onehot_columns(ids, count, base=0):
    place = lax.broadcasted_iota(jnp.int32, (count, ids.shape[1]), 0) + base
    return jnp.where(place == ids, 1.0, 0.0).astype(BF)


def rows(i, n):
    return pl.ds(pl.multiple_of(i * n, n), n)


def chunk(dx, dc):
    return pl.ds((dx * 2 + dc) * R, R)


def pair(dx):
    return pl.ds(dx * 2 * R, 2 * R)


def group(half, by, first=0, count=G):
    return pl.ds((ORDER.index(by) * 2 + half) * G + first, count)


def step_kernel(
    table_hbm, req_hbm, src_hbm, dst_hbm, lab_hbm, neg_hbm, ret, asked_out, rs2, part_out,
    table, req, src, dst, lab, neg, reqst, asked, picked, slots, cslots, cand, dnt, st, wt, cnt, off, cdeg,
    gneg, gst, opp, side, kept, gcown, rly, rs1, part, part_bf,
    in_sem, out_sem, s_req, r_req, s_slot, r_slot, s_ag1, r_ag1, s_ag2, r_ag2, s_ret, r_ret, s_rs1, r_rs1, s_rs2, r_rs2,
):
    e = lax.axis_index("eblock")
    d = lax.axis_index("dom")
    z, y = lax.div(e, 4), lax.rem(e, 4)
    x, c = lax.div(d, 2), lax.rem(d, 2)

    def plus(a, by, n=4):
        return lax.rem(a + by, n)

    def dom_peer(dx, dc):
        return plus(x, dx) * 2 + plus(c, dc, 2)

    def along(half, by):
        if half == 0:
            return (z * 4 + plus(y, by), d)
        return (plus(z, by) * 4 + y, d)

    def across(half, by):
        return along(1 - half, by)

    def remote(src, dst, ssem, rsem, to):
        return pltpu.make_async_remote_copy(
            src_ref=src, dst_ref=dst, send_sem=ssem, recv_sem=rsem, device_id=to, device_id_type=MESH
        )

    def local_copy(src, dst, sem):
        cp = pltpu.make_async_copy(src, dst, sem)
        cp.start()
        return cp

    barrier = pltpu.get_barrier_semaphore()
    for dx, dc in ((2, 0), (2, 1), (1, 0), (1, 1), (3, 0), (3, 1), (0, 1)):
        pl.semaphore_signal(barrier, inc=1, device_id=(e, dom_peer(dx, dc)), device_id_type=MESH)
    for by in RING:
        for half in range(2):
            pl.semaphore_signal(barrier, inc=1, device_id=along(half, by), device_id_type=MESH)

    loads = [
        local_copy(a, b, in_sem.at[i])
        for i, (a, b) in enumerate(
            ((req_hbm, req), (neg_hbm, neg), (table_hbm, table), (src_hbm, src), (dst_hbm, dst), (lab_hbm, lab))
        )
    ]
    loads[0].wait()
    for p in range(8):
        reqst[p] = jnp.broadcast_to(req[p : p + 1, :], (8, R))
    loads[1].wait()
    neg_hot = onehot_rows(jnp.broadcast_to(neg[...], (8, R)), V)
    pl.semaphore_wait(barrier, 13)

    req_cp = {}
    for i, (dx, dc) in enumerate(((2, 0), (2, 1), (1, 0), (1, 1), (3, 0), (3, 1), (0, 1))):
        peer = dom_peer(dx, dc)
        cp = remote(reqst.at[peer], asked.at[(4 - dx) % 4 * 2 + dc], s_req.at[i], r_req.at[i], (e, peer))
        cp.start()
        req_cp[dx, dc] = cp
    asked[0] = reqst[d]

    loads[2].wait()
    own = (nn(neg_hot, table[...]) * 0.5).astype(BF)
    ag1 = {}
    ag2 = {}

    def gather_step(half, k, to, by, first, count):
        cp = remote(
            cand.at[group(half, by, first, count)], cand.at[group(half, (by - to) % 4, first, count)],
            s_ag2.at[half * 14 + k], r_ag2.at[half * 14 + k], across(half, to),
        )
        cp.start()
        ag2[half, k] = cp

    for half in range(2):
        cand[group(half, 0, 0, H), :] = own[half * H : (half + 1) * H, :]
    def short_step(by):
        for half in range(2):
            k = half * 3 + RING.index(by)
            place = group(half, 0, ORDER.index((4 - by) % 4) * H, H)
            cp = remote(cand.at[group(half, 0, 0, H)], cand.at[place], s_ag1.at[k], r_ag1.at[k], along(half, by))
            cp.start()
            ag1[half, by] = cp

    short_step(1)
    short_step(3)
    for half in range(2):
        gather_step(half, 0, 1, 0, 0, H)
        gather_step(half, 1, 3, 0, 0, H)
    short_step(2)

    for cp in loads[3:]:
        cp.wait()
    weight = jnp.where(lab[...] == 1, LABEL, 1.0)
    line = lax.broadcasted_iota(jnp.int32, (R, E), 0)
    loop_weight = jnp.where(src[...] == dst[...], weight, 0.0)
    sums = jnp.where(line == 0, 1.0, jnp.where(line == 1, loop_weight, 0.0)).astype(BF)
    weight = weight.astype(BF)
    line = line.astype(F32).astype(BF)

    def incidence(t):
        at = rows(t, R)
        first = dom_peer(lax.div(t, 2), lax.rem(t, 2)) * R

        def ends(ids):
            place = ids[...] - first
            place = jnp.where((place >= 0) & (place < R), place, R).astype(F32).astype(BF)
            return jnp.where(line == place, jnp.ones((R, E), BF), jnp.zeros((R, E), BF))

        one = ends(src)
        both = one + ends(dst)
        st[at, :] = both.astype(BF)
        wt[at, :] = (both * weight).astype(BF)
        cdeg[at, :] = nt(one, sums)

    pl.loop(0, 4)(incidence)

    for cp in req_cp.values():
        cp.wait_recv()
    slot_cp = {}
    for dx in (1, 3, 2, 0):
        hot = jnp.concatenate([onehot_rows(asked[dx * 2], V), onehot_rows(asked[dx * 2 + 1], V)], axis=0)
        rows_out = nn(hot, table[...]).astype(BF)
        if dx == 0:
            slots[chunk(0, 0), :] = rows_out[:R, :]
            picked[chunk(0, 1), :] = rows_out[R:, :]
        else:
            picked[pair(dx), :] = rows_out
        for dc in range(2):
            if (dx, dc) == (0, 0):
                continue
            i = DOM.index((dx, dc))
            cp = remote(
                picked.at[chunk(dx, dc)], slots.at[chunk((4 - dx) % 4, dc)],
                s_slot.at[i], r_slot.at[i], (e, dom_peer(dx, dc)),
            )
            cp.start()
            slot_cp[dx, dc] = cp
    asked_cp = local_copy(asked, asked_out, out_sem.at[0])

    for half in range(2):
        for by in (1, 3):
            ag1[half, by].wait_recv()
    for half in range(2):
        gather_step(half, 2, 1, 0, H, H)
        gather_step(half, 3, 3, 0, 2 * H, H)
    for half in range(2):
        gather_step(half, 4, 1, 0, 2 * H, H)
        gather_step(half, 5, 3, 0, H, H)
    for half in range(2):
        ag2[half, 0].wait_recv()
        gather_step(half, 8, 1, 3, 0, H // 2)
        ag2[half, 1].wait_recv()
        gather_step(half, 9, 3, 1, H // 2, H // 2)
    pl.loop(4, 8)(incidence)
    for half in range(2):
        ag1[half, 2].wait_recv()
        gather_step(half, 6, 1, 0, 3 * H, H)
        gather_step(half, 7, 3, 0, 3 * H, H)

    def pair_counts(t):
        at = rows(t, 256)
        full = nt(st[at, :], wt[...])
        ones = jnp.floor(full * (1.0 / LABEL))
        many = full * 0.5 - (0.5 * LABEL - 0.5) * ones
        cnt[at, :] = many
        off[at, :] = many - ones
        alone = cdeg[at, 1:2]
        ones = jnp.floor(alone * (1.0 / LABEL))
        many = alone - (LABEL - 1.0) * ones
        same = lax.broadcasted_iota(jnp.int32, (256, 256), 0) == lax.broadcasted_iota(jnp.int32, (256, 256), 1)
        cnt[at, at] = jnp.where(same, many, cnt[at, at])
        off[at, at] = jnp.where(same, many - 2.0 * ones, off[at, at])

    pl.loop(0, 1)(pair_counts)

    for half in range(2):
        ag2[half, 2].wait_recv()
        gather_step(half, 10, 1, 3, H, H)
        ag2[half, 3].wait_recv()
        gather_step(half, 11, 3, 1, 2 * H, H)

    pl.loop(1, 3)(pair_counts)
    for half in range(2):
        ag2[half, 6].wait_recv()
        gather_step(half, 12, 1, 3, 3 * H, H // 2)
        ag2[half, 7].wait_recv()
        gather_step(half, 13, 3, 1, 3 * H + H // 2, H // 2)
    pl.loop(3, 4)(pair_counts)

    for half in range(2):
        for k in (4, 5):
            ag2[half, k].wait_recv()
    near, far = pl.ds(0, 6 * G), pl.ds(6 * G, 2 * G)
    lost = jnp.zeros((1, D), F32)

    def arrive(dx, lost):
        for dc in range(2):
            if (dx, dc) != (0, 0):
                slot_cp[(4 - dx) % 4, dc].wait_recv()
        at = pair(dx)
        many = slots[at, :].astype(F32) * (cdeg[at, :1] * (1.0 / 32))
        kept_many = many.astype(BF)
        cslots[at, :] = kept_many
        return lost + jnp.sum(many - kept_many.astype(F32), axis=0, keepdims=True)

    def score(dx, block, add):
        at = pair(dx)
        dneg = (jnp.tanh(nt(slots[at, :], cand[block, :])) + 1.0).astype(BF)
        more = nn(dneg, cand[block, :])
        gneg[at, :] = gneg[at, :] + more if add else more
        dnt[block, at] = jnp.transpose(dneg)

    for dx in (0, 1, 3, 2)[:3]:
        lost = arrive(dx, lost)
        score(dx, near, False)
    for half in range(2):
        for k in range(8, 14):
            ag2[half, k].wait_recv()
    for dx in (0, 1, 3, 2)[:3]:
        score(dx, far, True)
    lost = arrive((0, 1, 3, 2)[3], lost)
    score((0, 1, 3, 2)[3], far, False)

    ret_cp = []
    rs_cp = {}

    def slot_grads(dx):
        at = pair(dx)
        pos = nt(slots[at, :] * jnp.asarray(0.5, BF), slots[...])
        w = (cnt[at, :] * jnp.tanh(pos) + off[at, :]).astype(BF)
        gst[at, :] = (gneg[at, :] * (cdeg[at, :1] * (1.0 / 16)) + nn(w, slots[...])).astype(BF)
        for dc in range(2):
            if (dx, dc) == (0, 0):
                continue
            i = DOM.index((dx, dc))
            cp = remote(
                gst.at[chunk(dx, dc)], ret.at[chunk((4 - dx) % 4, dc)],
                s_ret.at[i], r_ret.at[i], (e, dom_peer(dx, dc)),
            )
            cp.start()
            ret_cp.append(cp)

    def cand_grads(half, by):
        return nn(dnt[group(half, by), :], cslots[...]) + lost

    def reduce_step(half, k, src, dst, to):
        cp = remote(src, dst, s_rs1.at[half * 6 + k], r_rs1.at[half * 6 + k], across(half, to))
        cp.start()
        rs_cp[half, k] = cp

    lo, hi = pl.ds(0, 2 * H), pl.ds(2 * H, 2 * H)
    sides = ((1, lo, hi, 0), (3, hi, lo, 1))

    def opposite(half):
        opp[half] = cand_grads(half, 2).astype(BF)
        reduce_step(half, 0, opp.at[half, lo], rly.at[half * 2], 1)
        reduce_step(half, 1, opp.at[half, hi], rly.at[half * 2 + 1], 3)

    def neighbours_early(half):
        for by, late, early, s in sides:
            n = half * 2 + s
            total = cand_grads(half, by)
            side[n] = total.astype(BF)
            kept[n] = total[2 * H * s : 2 * H * (s + 1), :]
            reduce_step(half, 2 + s, side.at[n, early], rs1.at[n, early], by)

    def neighbours_late(half):
        for by, late, early, s in sides:
            n = half * 2 + s
            rs_cp[half, s].wait_recv()
            side[n, late, :] = (kept[n] + rly[n].astype(F32)).astype(BF)
            reduce_step(half, 4 + s, side.at[n, late], rs1.at[n, late], by)

    def own_group(half):
        gcown[half] = cand_grads(half, 0)

    opposite(0)
    opposite(1)
    slot_grads(1)
    slot_grads(3)
    score(2, near, True)
    neighbours_early(0)
    neighbours_early(1)
    slot_grads(2)
    neighbours_late(0)
    neighbours_late(1)
    own_group(0)
    own_group(1)
    slot_grads(0)
    own_cp = local_copy(gst.at[chunk(0, 0)], ret.at[chunk(0, 0)], out_sem.at[1])
    for cps in (req_cp, ag1, ag2, slot_cp):
        for cp in cps.values():
            cp.wait_send()

    rs2_cp = []
    for half in range(2):
        for k in range(2, 6):
            rs_cp[half, k].wait_recv()
        total = gcown[half] + rs1[half * 2].astype(F32) + rs1[half * 2 + 1].astype(F32)
        part[half] = total[:H, :]
        part_bf[half] = total.astype(BF)
        for by in RING:
            k = half * 3 + RING.index(by)
            cp = remote(
                part_bf.at[half, pl.ds(ORDER.index(by) * H, H)], rs2.at[pl.ds(k * H, H)],
                s_rs2.at[k], r_rs2.at[k], along(half, by),
            )
            cp.start()
            rs2_cp.append(cp)
    part_cp = local_copy(part, part_out, out_sem.at[2])
    for cp in ret_cp:
        cp.wait_recv()
    for cp in rs2_cp:
        cp.wait_recv()

    for cp in (asked_cp, own_cp, part_cp):
        cp.wait()
    for cp in list(rs_cp.values()) + ret_cp + rs2_cp:
        cp.wait_send()


def scatter_kernel(
    ret_hbm, asked_hbm, neg_hbm, rs2_hbm, part_hbm, out_hbm, ret, asked, neg, rs2, part, out, in_sem, out_sem
):
    pairs = ((asked_hbm, asked), (ret_hbm, ret.at[pl.ds(0, S)]), (neg_hbm, neg), (rs2_hbm, rs2), (part_hbm, part))
    loads = []
    for i, (a, b) in enumerate(pairs):
        cp = pltpu.make_async_copy(a, b, in_sem.at[i])
        cp.start()
        loads.append(cp)
    loads[0].wait()
    loads[2].wait()
    line = lax.broadcasted_iota(jnp.int32, (256, R), 0).astype(F32).astype(BF)

    def hot(ids, first):
        place = ids - first
        place = jnp.where((place >= 0) & (place < 256), place, 256).astype(F32).astype(BF)
        return jnp.where(line == place, jnp.ones((256, R), BF), jnp.zeros((256, R), BF))

    hots = []
    for t in range(4):
        negs = hot(neg[...], t * 256)
        hots.append(jnp.concatenate([hot(asked[p, :1, :], t * 256) for p in range(8)] + [negs, negs], axis=1))
    loads[3].wait()
    loads[4].wait()
    for half in range(2):
        total = part[half]
        for i in range(3):
            k = half * 3 + i
            total = total + rs2[k * H : (k + 1) * H, :].astype(F32)
        high = total.astype(BF)
        ret[S + half * H : S + (half + 1) * H, :] = high
        ret[S + R + half * H : S + R + (half + 1) * H, :] = (total - high.astype(F32)).astype(BF)
    loads[1].wait()
    stores = []
    for t in range(4):
        at = pl.ds(t * 256, 256)
        out[at, :] = nn(hots[t], ret[...])
        cp = pltpu.make_async_copy(out.at[at], out_hbm.at[at], out_sem.at[t])
        cp.start()
        stores.append(cp)
    for cp in stores:
        cp.wait()


def local(table, requests, edge_src, edge_dst, labels, neg_ids):
    hbm = pl.BlockSpec(memory_space=pltpu.HBM)
    dma = pltpu.SemaphoreType.DMA
    negs = neg_ids.reshape(1, R)
    ids = pltpu.VMEM((1, E), jnp.int32)
    ret, asked, rs2, part = pl.pallas_call(
        step_kernel,
        out_shape=(
            jax.ShapeDtypeStruct((S, D), BF),
            jax.ShapeDtypeStruct((8, 8, R), jnp.int32),
            jax.ShapeDtypeStruct((6 * H, D), BF),
            jax.ShapeDtypeStruct((2, H, D), F32),
        ),
        in_specs=[hbm] * 6,
        out_specs=(hbm,) * 4,
        scratch_shapes=[
            pltpu.VMEM((V, D), BF),
            pltpu.VMEM((8, R), jnp.int32),
            ids, ids, ids,
            pltpu.VMEM((1, R), jnp.int32),
            pltpu.VMEM((8, 8, R), jnp.int32),
            pltpu.VMEM((8, 8, R), jnp.int32),
            pltpu.VMEM((S, D), BF),
            pltpu.VMEM((S, D), BF),
            pltpu.VMEM((S, D), BF),
            pltpu.VMEM((C, D), BF),
            pltpu.VMEM((C, S), BF),
            pltpu.VMEM((S, E), BF),
            pltpu.VMEM((S, E), BF),
            pltpu.VMEM((S, S), F32),
            pltpu.VMEM((S, S), F32),
            pltpu.VMEM((S, R), F32),
            pltpu.VMEM((S, D), F32),
            pltpu.VMEM((S, D), BF),
            pltpu.VMEM((2, G, D), BF),
            pltpu.VMEM((4, G, D), BF),
            pltpu.VMEM((4, 2 * H, D), F32),
            pltpu.VMEM((2, G, D), F32),
            pltpu.VMEM((4, 2 * H, D), BF),
            pltpu.VMEM((4, G, D), BF),
            pltpu.VMEM((2, H, D), F32),
            pltpu.VMEM((2, G, D), BF),
            dma((6,)), dma((3,)),
            dma((7,)), dma((7,)),
            dma((7,)), dma((7,)),
            dma((6,)), dma((6,)),
            dma((28,)), dma((28,)),
            dma((7,)), dma((7,)),
            dma((12,)), dma((12,)),
            dma((6,)), dma((6,)),
        ],
        compiler_params=pltpu.CompilerParams(
            collective_id=0, has_side_effects=True, vmem_limit_bytes=56 * 1024 * 1024
        ),
        name="link_step",
    )(
        table,
        requests.reshape(8, R),
        edge_src.reshape(1, E),
        edge_dst.reshape(1, E),
        labels.reshape(1, E),
        negs,
    )
    return pl.pallas_call(
        scatter_kernel,
        out_shape=jax.ShapeDtypeStruct((V, D), F32),
        in_specs=[hbm] * 5,
        out_specs=hbm,
        scratch_shapes=[
            pltpu.VMEM((S + 2 * R, D), BF),
            pltpu.VMEM((8, 8, R), jnp.int32),
            pltpu.VMEM((1, R), jnp.int32),
            pltpu.VMEM((6 * H, D), BF),
            pltpu.VMEM((2, H, D), F32),
            pltpu.VMEM((V, D), F32),
            dma((5,)), dma((4,)),
        ],
        compiler_params=pltpu.CompilerParams(vmem_limit_bytes=56 * 1024 * 1024),
        name="scatter",
    )(ret, asked, negs, rs2, part)


def solution(mesh):
    return jax.shard_map(
        local,
        mesh=mesh,
        in_specs=(
            P(("eblock", "dom"), None),
            P("eblock", "dom", None, None),
            P("eblock", "dom", None),
            P("eblock", "dom", None),
            P("eblock", "dom", None),
            P("eblock", "dom", None),
        ),
        out_specs=P(("eblock", "dom"), None),
        check_vma=False,
    )
```

```python
import jax
import jax.numpy as jnp
from jax import lax
from jax.experimental import pallas as pl
from jax.experimental.pallas import tpu as pltpu
from jax.sharding import PartitionSpec as P

MESH = pl.DeviceIdType.MESH
BF = jnp.bfloat16
F32 = jnp.float32
D = 512
R = 128
S = 1024
E = 2048
C = 2048
V = 1024
H = 64
G = 4 * H
LABEL = 4096.0

DOM = ((1, 0), (1, 1), (3, 0), (3, 1), (2, 0), (2, 1), (0, 1))
RING = (2, 1, 3)
ORDER = (0, 1, 3, 2)


def nt(a, b):
    return lax.dot_general(a, b, (((1,), (1,)), ((), ())), preferred_element_type=F32)


def nn(a, b):
    return jnp.dot(a, b, preferred_element_type=F32)


def onehot_rows(ids, count):
    column = jnp.transpose(ids)[:, :1]
    return jnp.where(lax.broadcasted_iota(jnp.int32, (R, count), 1) == column, 1.0, 0.0).astype(BF)


def onehot_columns(ids, count, base=0):
    place = lax.broadcasted_iota(jnp.int32, (count, ids.shape[1]), 0) + base
    return jnp.where(place == ids, 1.0, 0.0).astype(BF)


def rows(i, n):
    return pl.ds(pl.multiple_of(i * n, n), n)


def chunk(dx, dc):
    return pl.ds((dx * 2 + dc) * R, R)


def pair(dx):
    return pl.ds(dx * 2 * R, 2 * R)


def group(half, by, first=0, count=G):
    return pl.ds((ORDER.index(by) * 2 + half) * G + first, count)


def step_kernel(
    table_hbm, req_hbm, src_hbm, dst_hbm, lab_hbm, neg_hbm, ret, asked_out, rs2, part_out,
    table, req, src, dst, lab, neg, reqst, asked, picked, slots, cslots, cand, dnt, st, wt, cnt, off, cdeg,
    gneg, gst, opp, side, kept, gcown, rly, rs1, part, part_bf,
    in_sem, out_sem, s_req, r_req, s_slot, r_slot, s_ag1, r_ag1, s_ag2, r_ag2, s_ret, r_ret, s_rs1, r_rs1, s_rs2, r_rs2,
):
    e = lax.axis_index("eblock")
    d = lax.axis_index("dom")
    z, y = lax.div(e, 4), lax.rem(e, 4)
    x, c = lax.div(d, 2), lax.rem(d, 2)

    def plus(a, by, n=4):
        return lax.rem(a + by, n)

    def dom_peer(dx, dc):
        return plus(x, dx) * 2 + plus(c, dc, 2)

    def along(half, by):
        if half == 0:
            return (z * 4 + plus(y, by), d)
        return (plus(z, by) * 4 + y, d)

    def across(half, by):
        return along(1 - half, by)

    def remote(src, dst, ssem, rsem, to):
        return pltpu.make_async_remote_copy(
            src_ref=src, dst_ref=dst, send_sem=ssem, recv_sem=rsem, device_id=to, device_id_type=MESH
        )

    def local_copy(src, dst, sem):
        cp = pltpu.make_async_copy(src, dst, sem)
        cp.start()
        return cp

    barrier = pltpu.get_barrier_semaphore()
    for dx, dc in ((2, 0), (2, 1), (1, 0), (1, 1), (3, 0), (3, 1), (0, 1)):
        pl.semaphore_signal(barrier, inc=1, device_id=(e, dom_peer(dx, dc)), device_id_type=MESH)
    for by in RING:
        for half in range(2):
            pl.semaphore_signal(barrier, inc=1, device_id=along(half, by), device_id_type=MESH)

    loads = [
        local_copy(a, b, in_sem.at[i])
        for i, (a, b) in enumerate(
            ((req_hbm, req), (neg_hbm, neg), (table_hbm, table), (src_hbm, src), (dst_hbm, dst), (lab_hbm, lab))
        )
    ]
    loads[0].wait()
    for p in range(8):
        reqst[p] = jnp.broadcast_to(req[p : p + 1, :], (8, R))
    loads[1].wait()
    neg_hot = onehot_rows(jnp.broadcast_to(neg[...], (8, R)), V)
    pl.semaphore_wait(barrier, 13)

    req_cp = {}
    for i, (dx, dc) in enumerate(((2, 0), (2, 1), (1, 0), (1, 1), (3, 0), (3, 1), (0, 1))):
        peer = dom_peer(dx, dc)
        cp = remote(reqst.at[peer], asked.at[(4 - dx) % 4 * 2 + dc], s_req.at[i], r_req.at[i], (e, peer))
        cp.start()
        req_cp[dx, dc] = cp
    asked[0] = reqst[d]

    loads[2].wait()
    own = (nn(neg_hot, table[...]) * 0.5).astype(BF)
    ag1 = {}
    ag2 = {}

    def gather_step(half, k, to, by, first, count):
        cp = remote(
            cand.at[group(half, by, first, count)], cand.at[group(half, (by - to) % 4, first, count)],
            s_ag2.at[half * 14 + k], r_ag2.at[half * 14 + k], across(half, to),
        )
        cp.start()
        ag2[half, k] = cp

    for half in range(2):
        cand[group(half, 0, 0, H), :] = own[half * H : (half + 1) * H, :]
    def short_step(by):
        for half in range(2):
            k = half * 3 + RING.index(by)
            place = group(half, 0, ORDER.index((4 - by) % 4) * H, H)
            cp = remote(cand.at[group(half, 0, 0, H)], cand.at[place], s_ag1.at[k], r_ag1.at[k], along(half, by))
            cp.start()
            ag1[half, by] = cp

    short_step(1)
    short_step(3)
    for half in range(2):
        gather_step(half, 0, 1, 0, 0, H)
        gather_step(half, 1, 3, 0, 0, H)
    short_step(2)

    for cp in loads[3:]:
        cp.wait()
    weight = jnp.where(lab[...] == 1, LABEL, 1.0)
    line = lax.broadcasted_iota(jnp.int32, (R, E), 0)
    loop_weight = jnp.where(src[...] == dst[...], weight, 0.0)
    sums = jnp.where(line == 0, 1.0, jnp.where(line == 1, loop_weight, 0.0)).astype(BF)
    weight = weight.astype(BF)
    line = line.astype(F32).astype(BF)

    def incidence(t):
        at = rows(t, R)
        first = dom_peer(lax.div(t, 2), lax.rem(t, 2)) * R

        def ends(ids):
            place = ids[...] - first
            place = jnp.where((place >= 0) & (place < R), place, R).astype(F32).astype(BF)
            return jnp.where(line == place, jnp.ones((R, E), BF), jnp.zeros((R, E), BF))

        one = ends(src)
        both = one + ends(dst)
        st[at, :] = both.astype(BF)
        wt[at, :] = (both * weight).astype(BF)
        cdeg[at, :] = nt(one, sums)

    pl.loop(0, 4)(incidence)

    slot_cp = {}
    for dx in (1, 3, 2, 0):
        for dc in range(2):
            if (dx, dc) != (0, 0):
                req_cp[(4 - dx) % 4, dc].wait_recv()
        hot = jnp.concatenate([onehot_rows(asked[dx * 2], V), onehot_rows(asked[dx * 2 + 1], V)], axis=0)
        rows_out = nn(hot, table[...]).astype(BF)
        if dx == 0:
            slots[chunk(0, 0), :] = rows_out[:R, :]
            picked[chunk(0, 1), :] = rows_out[R:, :]
        else:
            picked[pair(dx), :] = rows_out
        for dc in range(2):
            if (dx, dc) == (0, 0):
                continue
            i = DOM.index((dx, dc))
            cp = remote(
                picked.at[chunk(dx, dc)], slots.at[chunk((4 - dx) % 4, dc)],
                s_slot.at[i], r_slot.at[i], (e, dom_peer(dx, dc)),
            )
            cp.start()
            slot_cp[dx, dc] = cp
    asked_cp = local_copy(asked, asked_out, out_sem.at[0])

    for half in range(2):
        for by in (1, 3):
            ag1[half, by].wait_recv()
    for half in range(2):
        gather_step(half, 2, 1, 0, H, H)
        gather_step(half, 3, 3, 0, 2 * H, H)
    for half in range(2):
        gather_step(half, 4, 1, 0, 2 * H, H)
        gather_step(half, 5, 3, 0, H, H)
    for half in range(2):
        ag2[half, 0].wait_recv()
        gather_step(half, 8, 1, 3, 0, H // 2)
        ag2[half, 1].wait_recv()
        gather_step(half, 9, 3, 1, H // 2, H // 2)
    pl.loop(4, 8)(incidence)
    for half in range(2):
        ag1[half, 2].wait_recv()
        gather_step(half, 6, 1, 0, 3 * H, H)
        gather_step(half, 7, 3, 0, 3 * H, H)

    def pair_counts(t):
        at = rows(t, 256)
        full = nt(st[at, :], wt[...])
        ones = jnp.floor(full * (1.0 / LABEL))
        many = full * 0.5 - (0.5 * LABEL - 0.5) * ones
        cnt[at, :] = many
        off[at, :] = many - ones
        alone = cdeg[at, 1:2]
        ones = jnp.floor(alone * (1.0 / LABEL))
        many = alone - (LABEL - 1.0) * ones
        same = lax.broadcasted_iota(jnp.int32, (256, 256), 0) == lax.broadcasted_iota(jnp.int32, (256, 256), 1)
        cnt[at, at] = jnp.where(same, many, cnt[at, at])
        off[at, at] = jnp.where(same, many - 2.0 * ones, off[at, at])

    pl.loop(0, 1)(pair_counts)

    for half in range(2):
        ag2[half, 2].wait_recv()
        gather_step(half, 10, 1, 3, H, H)
        ag2[half, 3].wait_recv()
        gather_step(half, 11, 3, 1, 2 * H, H)

    pl.loop(1, 3)(pair_counts)
    for half in range(2):
        ag2[half, 6].wait_recv()
        gather_step(half, 12, 1, 3, 3 * H, H // 2)
        ag2[half, 7].wait_recv()
        gather_step(half, 13, 3, 1, 3 * H + H // 2, H // 2)
    pl.loop(3, 4)(pair_counts)

    for half in range(2):
        for k in (4, 5):
            ag2[half, k].wait_recv()
    near, far = pl.ds(0, 6 * G), pl.ds(6 * G, 2 * G)
    lost = jnp.zeros((1, D), F32)

    def arrive(dx, lost):
        for dc in range(2):
            if (dx, dc) != (0, 0):
                slot_cp[(4 - dx) % 4, dc].wait_recv()
        at = pair(dx)
        many = slots[at, :].astype(F32) * (cdeg[at, :1] * (1.0 / 32))
        kept_many = many.astype(BF)
        cslots[at, :] = kept_many
        return lost + jnp.sum(many - kept_many.astype(F32), axis=0, keepdims=True)

    def score(dx, block, add):
        at = pair(dx)
        dneg = (jnp.tanh(nt(slots[at, :], cand[block, :])) + 1.0).astype(BF)
        more = nn(dneg, cand[block, :])
        gneg[at, :] = gneg[at, :] + more if add else more
        dnt[block, at] = jnp.transpose(dneg)

    for dx in (0, 1, 3, 2)[:3]:
        lost = arrive(dx, lost)
        score(dx, near, False)
    for half in range(2):
        for k in range(8, 14):
            ag2[half, k].wait_recv()
    for dx in (0, 1, 3, 2)[:3]:
        score(dx, far, True)
    lost = arrive((0, 1, 3, 2)[3], lost)
    score((0, 1, 3, 2)[3], far, False)

    ret_cp = []
    rs_cp = {}

    def slot_grads(dx):
        at = pair(dx)
        pos = nt(slots[at, :] * jnp.asarray(0.5, BF), slots[...])
        w = (cnt[at, :] * jnp.tanh(pos) + off[at, :]).astype(BF)
        gst[at, :] = (gneg[at, :] * (cdeg[at, :1] * (1.0 / 16)) + nn(w, slots[...])).astype(BF)
        for dc in range(2):
            if (dx, dc) == (0, 0):
                continue
            i = DOM.index((dx, dc))
            cp = remote(
                gst.at[chunk(dx, dc)], ret.at[chunk((4 - dx) % 4, dc)],
                s_ret.at[i], r_ret.at[i], (e, dom_peer(dx, dc)),
            )
            cp.start()
            ret_cp.append(cp)

    def cand_grads(half, by):
        return nn(dnt[group(half, by), :], cslots[...]) + lost

    def reduce_step(half, k, src, dst, to):
        cp = remote(src, dst, s_rs1.at[half * 6 + k], r_rs1.at[half * 6 + k], across(half, to))
        cp.start()
        rs_cp[half, k] = cp

    lo, hi = pl.ds(0, 2 * H), pl.ds(2 * H, 2 * H)
    sides = ((1, lo, hi, 0), (3, hi, lo, 1))

    def opposite(half):
        opp[half] = cand_grads(half, 2).astype(BF)
        reduce_step(half, 0, opp.at[half, lo], rly.at[half * 2], 1)
        reduce_step(half, 1, opp.at[half, hi], rly.at[half * 2 + 1], 3)

    def neighbours_early(half):
        for by, late, early, s in sides:
            n = half * 2 + s
            total = cand_grads(half, by)
            side[n] = total.astype(BF)
            kept[n] = total[2 * H * s : 2 * H * (s + 1), :]
            reduce_step(half, 2 + s, side.at[n, early], rs1.at[n, early], by)

    def neighbours_late(half):
        for by, late, early, s in sides:
            n = half * 2 + s
            rs_cp[half, s].wait_recv()
            side[n, late, :] = (kept[n] + rly[n].astype(F32)).astype(BF)
            reduce_step(half, 4 + s, side.at[n, late], rs1.at[n, late], by)

    def own_group(half):
        gcown[half] = cand_grads(half, 0)

    opposite(0)
    opposite(1)
    slot_grads(1)
    slot_grads(3)
    score(2, near, True)
    neighbours_early(0)
    neighbours_early(1)
    slot_grads(2)
    neighbours_late(0)
    neighbours_late(1)
    own_group(0)
    own_group(1)
    slot_grads(0)
    own_cp = local_copy(gst.at[chunk(0, 0)], ret.at[chunk(0, 0)], out_sem.at[1])
    for cps in (req_cp, ag1, ag2, slot_cp):
        for cp in cps.values():
            cp.wait_send()

    rs2_cp = []
    for half in range(2):
        for k in range(2, 6):
            rs_cp[half, k].wait_recv()
        total = gcown[half] + rs1[half * 2].astype(F32) + rs1[half * 2 + 1].astype(F32)
        part[half] = total[:H, :]
        part_bf[half] = total.astype(BF)
        for by in RING:
            k = half * 3 + RING.index(by)
            cp = remote(
                part_bf.at[half, pl.ds(ORDER.index(by) * H, H)], rs2.at[pl.ds(k * H, H)],
                s_rs2.at[k], r_rs2.at[k], along(half, by),
            )
            cp.start()
            rs2_cp.append(cp)
    part_cp = local_copy(part, part_out, out_sem.at[2])
    for cp in ret_cp:
        cp.wait_recv()
    for cp in rs2_cp:
        cp.wait_recv()

    for cp in (asked_cp, own_cp, part_cp):
        cp.wait()
    for cp in list(rs_cp.values()) + ret_cp + rs2_cp:
        cp.wait_send()


def scatter_kernel(
    ret_hbm, asked_hbm, neg_hbm, rs2_hbm, part_hbm, out_hbm, ret, asked, neg, rs2, part, out, in_sem, out_sem
):
    pairs = ((asked_hbm, asked), (ret_hbm, ret.at[pl.ds(0, S)]), (neg_hbm, neg), (rs2_hbm, rs2), (part_hbm, part))
    loads = []
    for i, (a, b) in enumerate(pairs):
        cp = pltpu.make_async_copy(a, b, in_sem.at[i])
        cp.start()
        loads.append(cp)
    loads[0].wait()
    loads[2].wait()
    line = lax.broadcasted_iota(jnp.int32, (256, R), 0).astype(F32).astype(BF)

    def hot(ids, first):
        place = ids - first
        place = jnp.where((place >= 0) & (place < 256), place, 256).astype(F32).astype(BF)
        return jnp.where(line == place, jnp.ones((256, R), BF), jnp.zeros((256, R), BF))

    hots = []
    for t in range(4):
        negs = hot(neg[...], t * 256)
        hots.append(jnp.concatenate([hot(asked[p, :1, :], t * 256) for p in range(8)] + [negs, negs], axis=1))
    loads[3].wait()
    loads[4].wait()
    for half in range(2):
        total = part[half]
        for i in range(3):
            k = half * 3 + i
            total = total + rs2[k * H : (k + 1) * H, :].astype(F32)
        high = total.astype(BF)
        ret[S + half * H : S + (half + 1) * H, :] = high
        ret[S + R + half * H : S + R + (half + 1) * H, :] = (total - high.astype(F32)).astype(BF)
    loads[1].wait()
    stores = []
    for t in range(4):
        at = pl.ds(t * 256, 256)
        out[at, :] = nn(hots[t], ret[...])
        cp = pltpu.make_async_copy(out.at[at], out_hbm.at[at], out_sem.at[t])
        cp.start()
        stores.append(cp)
    for cp in stores:
        cp.wait()


def local(table, requests, edge_src, edge_dst, labels, neg_ids):
    hbm = pl.BlockSpec(memory_space=pltpu.HBM)
    dma = pltpu.SemaphoreType.DMA
    negs = neg_ids.reshape(1, R)
    ids = pltpu.VMEM((1, E), jnp.int32)
    ret, asked, rs2, part = pl.pallas_call(
        step_kernel,
        out_shape=(
            jax.ShapeDtypeStruct((S, D), BF),
            jax.ShapeDtypeStruct((8, 8, R), jnp.int32),
            jax.ShapeDtypeStruct((6 * H, D), BF),
            jax.ShapeDtypeStruct((2, H, D), F32),
        ),
        in_specs=[hbm] * 6,
        out_specs=(hbm,) * 4,
        scratch_shapes=[
            pltpu.VMEM((V, D), BF),
            pltpu.VMEM((8, R), jnp.int32),
            ids, ids, ids,
            pltpu.VMEM((1, R), jnp.int32),
            pltpu.VMEM((8, 8, R), jnp.int32),
            pltpu.VMEM((8, 8, R), jnp.int32),
            pltpu.VMEM((S, D), BF),
            pltpu.VMEM((S, D), BF),
            pltpu.VMEM((S, D), BF),
            pltpu.VMEM((C, D), BF),
            pltpu.VMEM((C, S), BF),
            pltpu.VMEM((S, E), BF),
            pltpu.VMEM((S, E), BF),
            pltpu.VMEM((S, S), F32),
            pltpu.VMEM((S, S), F32),
            pltpu.VMEM((S, R), F32),
            pltpu.VMEM((S, D), F32),
            pltpu.VMEM((S, D), BF),
            pltpu.VMEM((2, G, D), BF),
            pltpu.VMEM((4, G, D), BF),
            pltpu.VMEM((4, 2 * H, D), F32),
            pltpu.VMEM((2, G, D), F32),
            pltpu.VMEM((4, 2 * H, D), BF),
            pltpu.VMEM((4, G, D), BF),
            pltpu.VMEM((2, H, D), F32),
            pltpu.VMEM((2, G, D), BF),
            dma((6,)), dma((3,)),
            dma((7,)), dma((7,)),
            dma((7,)), dma((7,)),
            dma((6,)), dma((6,)),
            dma((28,)), dma((28,)),
            dma((7,)), dma((7,)),
            dma((12,)), dma((12,)),
            dma((6,)), dma((6,)),
        ],
        compiler_params=pltpu.CompilerParams(
            collective_id=0, has_side_effects=True, vmem_limit_bytes=56 * 1024 * 1024
        ),
        name="link_step",
    )(
        table,
        requests.reshape(8, R),
        edge_src.reshape(1, E),
        edge_dst.reshape(1, E),
        labels.reshape(1, E),
        negs,
    )
    return pl.pallas_call(
        scatter_kernel,
        out_shape=jax.ShapeDtypeStruct((V, D), F32),
        in_specs=[hbm] * 5,
        out_specs=hbm,
        scratch_shapes=[
            pltpu.VMEM((S + 2 * R, D), BF),
            pltpu.VMEM((8, 8, R), jnp.int32),
            pltpu.VMEM((1, R), jnp.int32),
            pltpu.VMEM((6 * H, D), BF),
            pltpu.VMEM((2, H, D), F32),
            pltpu.VMEM((V, D), F32),
            dma((5,)), dma((4,)),
        ],
        compiler_params=pltpu.CompilerParams(vmem_limit_bytes=56 * 1024 * 1024),
        name="scatter",
    )(ret, asked, negs, rs2, part)


def solution(mesh):
    return jax.shard_map(
        local,
        mesh=mesh,
        in_specs=(
            P(("eblock", "dom"), None),
            P("eblock", "dom", None, None),
            P("eblock", "dom", None),
            P("eblock", "dom", None),
            P("eblock", "dom", None),
            P("eblock", "dom", None),
        ),
        out_specs=P(("eblock", "dom"), None),
        check_vma=False,
    )
```
